32 devices in a mesh: section: 8 (over y, x, core), peer: 4 (over z).
Axes of the slice: x: 2, y: 2, z: 4, core: 2. Of those that a mesh axis runs over, the one named last changes fastest.
Arguments:
- stash: bfloat16 [8, 4, 3, 8, 5120], P('section', 'peer'), may hold values from -134 to 134
- back_in: bfloat16 [8, 4, 3, 8, 5120], P('section', 'peer'), may hold values from -6 to 6
- down_proj: bfloat16 [8, 144, 5120], P('section'), may hold values from -0.078125 to 0.078125
- up_proj: bfloat16 [8, 144, 5120], P('section'), may hold values from -0.5 to 0.5
- gain: float32 [8, 5120], P('section'), may hold values from 0.5 to 1.5
- sent_to: int32 [8, 4, 3], P('section', 'peer'), may hold values from 0 to 3, as said below
- sent_count: int32 [8, 4], P('section', 'peer'), may hold values from 2 to 3, as said below
- recv_from: int32 [8, 4, 3], P('section', 'peer'), may hold values from 0 to 3, as said below
- back_live: int32 [8, 4, 3], P('section', 'peer'), may hold values from 0 to 1, as said below
Outputs:
- returned: bfloat16 [8, 4, 3, 8, 5120], P('section', 'peer')
- grad_down: bfloat16 [8, 144, 5120], P('section')
- grad_up: bfloat16 [8, 144, 5120], P('section')
The draws below stay inside these ranges and needn't reach their ends.
Inputs may be any that keep to these rules, and one draw needn't show every extreme that they name: `sent_to`: the 3 slots of one device name distinct peers. `sent_count`: uneven over peers; on every section some peer has 3. `recv_from`: the 3 slots of one device name distinct peers. Peer c of section s - 1 (the last section before section 0) names peer a of section s in one of its first sent_count slots exactly when some slot of recv_from at (s, a) names c with back_live 1. `back_live`: on every section some device has all 3 slots live.
All inputs are finite; a program needn't handle non-finite values.
Results may differ from the reference program's by a relative error of at most 0.028.
Values may be sent and summed in bfloat16 or wider, within the bound.
A program may use at most 64 MiB of HBM per device.

```python
import math
import jax
import jax.numpy as jnp
from jax import lax

D = 5120
RANK = 144
MB = 8
SEND = 3
N_SECTION = 8
N_PEER = 4


def wiring(key):
    key_off = jax.random.fold_in(key, 101)
    key_order = jax.random.fold_in(key, 102)
    key_count = jax.random.fold_in(key, 103)
    key_full = jax.random.fold_in(key, 104)
    key_recv = jax.random.fold_in(key, 105)
    peer_index = jnp.arange(N_PEER, dtype=jnp.int32)
    slot_index = jnp.arange(SEND, dtype=jnp.int32)
    off_scores = jax.random.randint(key_off, (N_SECTION, N_PEER), 0, 2 ** 20) * N_PEER + peer_index[None, :]
    unused, offsets = lax.top_k(off_scores, SEND)
    offsets = offsets.astype(jnp.int32)
    order_scores = jax.random.randint(key_order, (N_SECTION, N_PEER, SEND), 0, 2 ** 20) * SEND + slot_index[None, None, :]
    unused, order = lax.top_k(order_scores, SEND)
    order = order.astype(jnp.int32)
    full_recv = jax.random.randint(key_recv, (N_SECTION,), 0, N_PEER).astype(jnp.int32)
    needed = (full_recv[:, None] - peer_index[None, :]) % N_PEER
    match = offsets[:, None, :] == needed[:, :, None]
    found = jnp.any(match, axis=2)
    wanted = jnp.sum(match.astype(jnp.int32) * slot_index[None, None, :], axis=2).astype(jnp.int32)
    first = order[:, :, 0]
    swapped = jnp.where(order == wanted[:, :, None], first[:, :, None], jnp.where(slot_index[None, None, :] == 0, wanted[:, :, None], order))
    order = jnp.where(found[:, :, None], swapped, order).astype(jnp.int32)
    lowest = max(1, SEND - max(1, SEND // 4))
    live_count = jax.random.randint(key_count, (N_SECTION, N_PEER), lowest, SEND + 1)
    full_peer = jax.random.randint(key_full, (N_SECTION,), 0, N_PEER)
    live_count = jnp.where(peer_index[None, :] == full_peer[:, None], SEND, live_count).astype(jnp.int32)
    offsets_wide = jnp.broadcast_to(offsets[:, None, :], (N_SECTION, N_PEER, SEND))
    picked = jnp.take_along_axis(offsets_wide, order, axis=2)
    routes = ((peer_index[None, :, None] + picked) % N_PEER).astype(jnp.int32)
    position = jnp.sum((order[:, :, :, None] == slot_index[None, None, None, :]).astype(jnp.int32) * slot_index[None, None, :, None], axis=2)
    live_send = (position < live_count[:, :, None]).astype(jnp.int32)
    senders = ((peer_index[None, :, None] - offsets[:, None, :]) % N_PEER).astype(jnp.int32)
    live_recv = jnp.take_along_axis(live_send, senders, axis=1)
    recv_from = jnp.roll(senders, 1, axis=0).astype(jnp.int32)
    back_live = jnp.roll(live_recv, 1, axis=0).astype(jnp.int32)
    return (routes, live_count, recv_from, back_live)


def draw_sent_to(key, part):
    routes, live_count, recv_from, back_live = wiring(key)
    return routes


def draw_sent_count(key, part):
    routes, live_count, recv_from, back_live = wiring(key)
    return live_count


def draw_recv_from(key, part):
    routes, live_count, recv_from, back_live = wiring(key)
    return recv_from


def draw_back_live(key, part):
    routes, live_count, recv_from, back_live = wiring(key)
    return back_live


def draw_stash(key, part):
    key = jax.random.fold_in(key, 11)
    key_base = jax.random.fold_in(key, 1)
    key_column = jax.random.fold_in(key, 2)
    key_row = jax.random.fold_in(key, 3)
    shape = (N_SECTION, N_PEER, SEND, MB, D)
    column = jnp.exp(jax.random.uniform(key_column, (N_SECTION, 1, 1, 1, D), dtype=jnp.float32) * math.log(10.0))
    rowscale = jnp.exp(jax.random.uniform(key_row, (N_SECTION, N_PEER, SEND, MB, 1), dtype=jnp.float32) * math.log(10.0))
    base = jax.random.truncated_normal(key_base, -4.0, 4.0, shape, dtype=jnp.float32)
    return (base * column * rowscale / 3.0).astype(jnp.bfloat16)


def block_levels(rng, dims, pieces, low, largest):
    level, own = 1.0, jax.random.fold_in(rng, 6)
    for dim, blocks in pieces:
        draws = jnp.exp(jax.random.uniform(jax.random.fold_in(own, dim), (blocks,), jnp.float32, low / len(pieces), largest / len(pieces)))
        level = level * jnp.repeat(draws, dims[dim] // blocks).reshape([-1 if axis == dim else 1 for axis in range(len(dims))])
    return level


def scatter_about(rng, dims, width, bound, cuts=(), held_as=jnp.bfloat16):
    drawn = jax.random.normal(rng, dims, jnp.float32) * width
    if len(cuts) > 0:
        drawn = block_levels(rng, dims, cuts, -0.22, 0.18) * drawn
    return jnp.clip(drawn, min=-bound, max=bound).astype(held_as)


def setup_inputs(seed: int = 0) -> dict:
    arg_keys = jax.random.split(jax.random.key(seed), 10)
    return {
        "stash": draw_stash(jax.random.fold_in(arg_keys[9], 71), 0),
        "back_in": scatter_about(arg_keys[1], (N_SECTION, N_PEER, SEND, MB, D), 1.0, 6.0, ((0, 8), (1, 4))),
        "down_proj": scatter_about(arg_keys[2], (N_SECTION, RANK, D), D ** -0.5, 0.078125, ((0, 8),)),
        "up_proj": scatter_about(arg_keys[3], (N_SECTION, RANK, D), RANK ** -0.5, 0.5, ((0, 8),)),
        "gain": jnp.clip(1.0 + 0.1 * jax.random.normal(arg_keys[4], (N_SECTION, D), jnp.float32), 0.5, 1.5),
        "sent_to": draw_sent_to(jax.random.fold_in(arg_keys[9], 71), 0),
        "sent_count": draw_sent_count(jax.random.fold_in(arg_keys[9], 71), 0),
        "recv_from": draw_recv_from(jax.random.fold_in(arg_keys[9], 71), 0),
        "back_live": draw_back_live(jax.random.fold_in(arg_keys[9], 71), 0),
    }


epsilon = 1e-05

def section_backward(items):
    stash, back_in, back_live, recv_from, down_proj, up_proj, gain, prev_sent, prev_count = items
    slot_mask = back_live.astype(jnp.bfloat16)[:, :, None, None]
    stored = stash * slot_mask
    incoming = back_in * slot_mask
    peer_count, slot_count, micro_rows, model_width = stored.shape
    stored = stored.reshape(peer_count, slot_count * micro_rows, model_width)
    incoming = incoming.reshape(peer_count, slot_count * micro_rows, model_width)
    stored_f = stored.astype(jnp.float32)
    inverse = lax.rsqrt(lax.optimization_barrier(jnp.mean(stored_f * stored_f, axis=-1, keepdims=True)) + epsilon)
    unit_rows = stored_f * inverse
    normed = (unit_rows * gain).astype(jnp.bfloat16)
    down_f = down_proj.astype(jnp.float32)
    up_f = up_proj.astype(jnp.float32)
    preact = jnp.einsum('prd,kd->prk', normed.astype(jnp.float32), down_f)
    sigmoid_pre = jax.nn.sigmoid(preact)
    activation = (preact * sigmoid_pre).astype(jnp.bfloat16)
    incoming_f = incoming.astype(jnp.float32)
    back_act = jnp.einsum('prd,kd->prk', incoming_f, up_f)
    back_pre = (back_act * (sigmoid_pre * (1.0 + preact * (1.0 - sigmoid_pre)))).astype(jnp.bfloat16)
    back_norm = jnp.einsum('prk,kd->prd', back_pre.astype(jnp.float32), down_f) * gain
    input_grad = incoming_f + inverse * (back_norm - unit_rows * lax.optimization_barrier(jnp.mean(back_norm * unit_rows, axis=-1, keepdims=True)))
    input_grad = input_grad.astype(jnp.bfloat16)
    part_down = jnp.einsum('prk,prd->pkd', back_pre.astype(jnp.float32), normed.astype(jnp.float32)).astype(jnp.bfloat16)
    part_up = jnp.einsum('prk,prd->pkd', activation.astype(jnp.float32), incoming_f).astype(jnp.bfloat16)
    grad_down = (lax.optimization_barrier(jnp.sum(part_down.astype(jnp.float32), axis=0)) / peer_count).astype(jnp.bfloat16)
    grad_up = (lax.optimization_barrier(jnp.sum(part_up.astype(jnp.float32), axis=0)) / peer_count).astype(jnp.bfloat16)
    input_grad = input_grad.reshape(peer_count, slot_count, micro_rows, model_width)
    peer_index = jnp.arange(peer_count, dtype=jnp.int32)
    onehot = ((recv_from.astype(jnp.int32)[:, :, None] == peer_index[None, None, :]) & (back_live[:, :, None] == 1)).astype(jnp.float32)
    by_sender = jnp.einsum('arc,armd->acmd', onehot, input_grad.astype(jnp.float32)).astype(jnp.bfloat16)
    swapped = jnp.swapaxes(by_sender, 0, 1)
    picked = jnp.take_along_axis(swapped, prev_sent.astype(jnp.int32)[:, :, None, None], axis=1)
    send_slots = prev_sent.shape[1]
    live_mask = (jnp.arange(send_slots, dtype=jnp.int32)[None, :] < prev_count[:, None]).astype(jnp.bfloat16)
    return (picked * live_mask[:, :, None, None], grad_down, grad_up)

def reference(stash, back_in, down_proj, up_proj, gain, sent_to, sent_count, recv_from, back_live):
    prev_sent = jnp.roll(sent_to, 1, axis=0)
    prev_count = jnp.roll(sent_count, 1, axis=0)
    shifted, grad_down, grad_up = lax.map(section_backward, (stash, back_in, back_live, recv_from, down_proj, up_proj, gain, prev_sent, prev_count))
    returned = jnp.roll(shifted, -1, axis=0)
    return (returned, grad_down, grad_up)
```

```python
import functools

import jax
import jax.numpy as jnp
from jax import lax
from jax.experimental import pallas as pl
from jax.experimental.pallas import tpu as pltpu
from jax.sharding import PartitionSpec as P

MESH = pl.DeviceIdType.MESH
LANES = 128
WIDE = 256

epsilon = 1e-05


def passed_along(block, axis, distance):
    devices = range(lax.axis_size(axis))
    route = [((i - distance) % len(devices), i) for i in devices]
    return lax.ppermute(block, axis, route)


def compact(blocks, targets, live_count):
    peer_count = blocks.shape[0]
    send_slots = targets.shape[0]
    peer_index = jnp.arange(peer_count, dtype=jnp.int32)
    slot_index = jnp.arange(send_slots, dtype=jnp.int32)
    selector = (
        (targets[:, None] == peer_index[None, :]) & (slot_index[:, None] < live_count)
    ).astype(jnp.bfloat16)
    flat = blocks.reshape(peer_count, -1)
    packed = jnp.dot(selector, flat, preferred_element_type=jnp.float32).astype(jnp.bfloat16)
    return packed.reshape((send_slots,) + blocks.shape[1:])


def on_device(stash, back_in, down_proj, up_proj, gain, sent_to, sent_count, recv_from, back_live):
    peer_count = lax.axis_size("peer")
    live_slots = back_live[0, 0]
    slot_mask = live_slots.astype(jnp.bfloat16)[:, None, None]
    slot_count = stash.shape[2]
    micro_rows = stash.shape[3]
    model_width = stash.shape[4]
    stored = (stash[0, 0] * slot_mask).reshape(slot_count * micro_rows, model_width)
    incoming = (back_in[0, 0] * slot_mask).reshape(slot_count * micro_rows, model_width)
    section_gain = gain[0]
    down_local = down_proj[0]
    up_local = up_proj[0]
    stored_f = stored.astype(jnp.float32)
    inverse = lax.rsqrt(jnp.mean(stored_f * stored_f, axis=-1, keepdims=True) + epsilon)
    unit_rows = stored_f * inverse
    normed = (unit_rows * section_gain).astype(jnp.bfloat16)
    contract_last = (((1,), (1,)), ((), ()))
    contract_rows = (((0,), (0,)), ((), ()))
    preact = lax.dot_general(normed, down_local, contract_last, preferred_element_type=jnp.float32)
    sigmoid_pre = jax.nn.sigmoid(preact)
    activation = (preact * sigmoid_pre).astype(jnp.bfloat16)
    back_act = lax.dot_general(
        incoming, up_local, contract_last, preferred_element_type=jnp.float32
    )
    back_pre = (back_act * (sigmoid_pre * (1.0 + preact * (1.0 - sigmoid_pre)))).astype(
        jnp.bfloat16
    )
    back_norm = jnp.dot(back_pre, down_local, preferred_element_type=jnp.float32) * section_gain
    input_grad = incoming.astype(jnp.float32) + inverse * (
        back_norm - unit_rows * jnp.mean(back_norm * unit_rows, axis=-1, keepdims=True)
    )
    input_grad = input_grad.astype(jnp.bfloat16)
    peer_index = jnp.arange(peer_count, dtype=jnp.int32)
    spreader = (
        (recv_from[0, 0][None, :] == peer_index[:, None]) & (live_slots[None, :] == 1)
    ).astype(jnp.bfloat16)
    by_sender = jnp.dot(
        spreader, input_grad.reshape(slot_count, -1), preferred_element_type=jnp.float32
    ).astype(jnp.bfloat16)
    by_sender = by_sender.reshape(peer_count, micro_rows, model_width)
    exchanged = lax.all_to_all(by_sender, "peer", split_axis=0, concat_axis=0, tiled=True)
    arrived = passed_along(exchanged, "section", -1)
    returned = compact(arrived, sent_to[0, 0], sent_count[0, 0])
    part_down = (
        lax.dot_general(back_pre, normed, contract_rows, preferred_element_type=jnp.float32)
        .astype(jnp.bfloat16)
        .astype(jnp.float32)
    )
    part_up = (
        lax.dot_general(activation, incoming, contract_rows, preferred_element_type=jnp.float32)
        .astype(jnp.bfloat16)
        .astype(jnp.float32)
    )
    summed_down, summed_up = (
        lax.psum(part_down.astype(jnp.bfloat16), "peer").astype(jnp.float32),
        lax.psum(part_up.astype(jnp.bfloat16), "peer").astype(jnp.float32),
    )
    grad_down = (summed_down / peer_count).astype(jnp.bfloat16)
    grad_up = (summed_up / peer_count).astype(jnp.bfloat16)
    return (returned[None, None], grad_down[None], grad_up[None])


def gather_kernel(
    sections,
    n,
    parts,
    stash,
    back_in,
    down,
    up,
    gain_ref,
    sent_to,
    sent_count,
    recv_from,
    back_live,
    returned,
    grad_down,
    grad_up,
    rows_all,
    factors,
    w_down,
    w_up,
    asked,
    wanted,
    picked,
    local_sem,
    right_sem,
    left_sem,
    recv_sem,
    fac_right,
    fac_left,
    fac_recv,
    want_sem,
    back_send,
    back_recv,
):
    section = lax.axis_index("section")
    me = lax.axis_index("peer")
    before = lax.rem(section + sections - 1, sections)
    after = lax.rem(section + 1, sections)
    rows, width = stash.shape
    rank = down.shape[0]
    part = width // parts
    has_left, has_right = me > 0, me < n - 1

    def cols(j):
        return pl.ds(pl.multiple_of(j * part, part), part)

    def along(origin, kind, j, step, own=False):
        view = rows_all.at[origin, kind, :, cols(j)]
        source = (stash, back_in)[kind].at[:, cols(j)] if own else view
        return pltpu.make_async_remote_copy(
            src_ref=source,
            dst_ref=view,
            send_sem=(right_sem if step > 0 else left_sem).at[origin, kind, j],
            recv_sem=recv_sem.at[origin, kind, j],
            device_id=(section, me + step),
            device_id_type=MESH,
        )

    def factor_along(origin, step):
        return pltpu.make_async_remote_copy(
            src_ref=factors.at[origin],
            dst_ref=factors.at[origin],
            send_sem=(fac_right if step > 0 else fac_left).at[origin],
            recv_sem=fac_recv.at[origin],
            device_id=(section, me + step),
            device_id_type=MESH,
        )

    def want_copy():
        return pltpu.make_async_remote_copy(
            src_ref=asked,
            dst_ref=wanted,
            send_sem=want_sem.at[0],
            recv_sem=want_sem.at[1],
            device_id=(after, me),
            device_id_type=MESH,
        )

    def back_copy(j):
        return pltpu.make_async_remote_copy(
            src_ref=picked.at[:, cols(j)],
            dst_ref=returned.at[:, cols(j)],
            send_sem=back_send.at[j],
            recv_sem=back_recv.at[j],
            device_id=(before, me),
            device_id_type=MESH,
        )

    loads = [
        pltpu.make_async_copy(stash, rows_all.at[me, 0], local_sem.at[0]),
        pltpu.make_async_copy(back_in, rows_all.at[me, 1], local_sem.at[1]),
        pltpu.make_async_copy(down, w_down.at[pl.ds(0, rank)], local_sem.at[2]),
        pltpu.make_async_copy(up, w_up.at[pl.ds(0, rank)], local_sem.at[3]),
    ]
    for load in loads:
        load.start()

    barrier = pltpu.get_barrier_semaphore()
    for other in (before, after):
        pl.semaphore_signal(barrier, inc=1, device_id=(other, me), device_id_type=MESH)

    @pl.when(has_left)
    def _():
        pl.semaphore_signal(barrier, inc=1, device_id=(section, me - 1), device_id_type=MESH)

    @pl.when(has_right)
    def _():
        pl.semaphore_signal(barrier, inc=1, device_id=(section, me + 1), device_id_type=MESH)

    @pl.when(has_left & has_right)
    def _():
        pl.semaphore_wait(barrier, 4)

    @pl.when(jnp.logical_not(has_left & has_right))
    def _():
        pl.semaphore_wait(barrier, 3)

    for j in range(parts):
        for kind in (0, 1):

            @pl.when(has_right)
            def _(j=j, kind=kind):
                along(me, kind, j, 1, True).start()

            @pl.when(has_left)
            def _(j=j, kind=kind):
                along(me, kind, j, -1, True).start()

    slots = sent_to.shape[2]
    micro = rows // slots
    at_row = lax.broadcasted_iota(jnp.int32, (rows, LANES), 0)
    at_lane = lax.broadcasted_iota(jnp.int32, (rows, LANES), 1)
    lane_peer = jnp.zeros((rows, LANES), jnp.int32)
    for a in range(1, n):
        lane_peer += jnp.where(at_lane >= a * rows, 1, 0)
    target = jnp.full((rows, LANES), -1, jnp.int32)
    for k in range(slots):
        here = (at_row >= k * micro) & (at_row < (k + 1) * micro)
        target = jnp.where(here & (sent_count[0, 0] > k), sent_to[0, 0, k], target)
    same = lax.rem(at_lane, micro) == lax.rem(at_row, micro)
    asked[...] = jnp.where(same & (lane_peer == target), 1.0, 0.0)
    want_copy().start()

    w_down[pl.ds(rank, WIDE - rank), :] = jnp.zeros((WIDE - rank, width), jnp.bfloat16)
    w_up[pl.ds(rank, WIDE - rank), :] = jnp.zeros((WIDE - rank, width), jnp.bfloat16)
    for load in loads:
        load.wait()

    def square_part(j, total):
        block = rows_all[me, 0, :, cols(j)].astype(jnp.float32)
        return total + jnp.sum(block * block, axis=-1, keepdims=True)

    squares = lax.fori_loop(0, parts, square_part, jnp.zeros((rows, 1), jnp.float32))
    inverse = lax.rsqrt(squares / width + epsilon)
    contract_last = (((1,), (1,)), ((), ()))

    def project_part(j, carry):
        pre, back = carry
        block = rows_all[me, 0, :, cols(j)].astype(jnp.float32)
        normed = (block * inverse * gain_ref[:, cols(j)]).astype(jnp.bfloat16)
        pre = pre + lax.dot_general(
            normed, w_down[:, cols(j)], contract_last, preferred_element_type=jnp.float32
        )
        back = back + lax.dot_general(
            rows_all[me, 1, :, cols(j)],
            w_up[:, cols(j)],
            contract_last,
            preferred_element_type=jnp.float32,
        )
        return pre, back

    empty = jnp.zeros((rows, WIDE), jnp.float32)
    preact, back_act = lax.fori_loop(0, parts, project_part, (empty, empty))
    row_only = lax.broadcasted_iota(jnp.int32, (rows, 1), 0)
    code_lane = lax.broadcasted_iota(jnp.int32, (8, LANES), 1) - me * rows
    live = jnp.zeros((rows, 1), jnp.float32)
    codes = jnp.zeros((8, LANES), jnp.float32)
    for k in range(slots):
        held = back_live[0, 0, k]
        here = (row_only >= k * micro) & (row_only < (k + 1) * micro)
        live = jnp.where(here, held.astype(jnp.float32), live)
        here = (code_lane >= k * micro) & (code_lane < (k + 1) * micro)
        codes = jnp.where(here, ((recv_from[0, 0, k] + 1) * held).astype(jnp.float32), codes)
    sigmoid_pre = jax.nn.sigmoid(preact)
    activation = preact * sigmoid_pre * live
    back_pre = back_act * (sigmoid_pre * (1.0 + preact * (1.0 - sigmoid_pre))) * live
    slope = jnp.sum(back_pre * preact, axis=-1, keepdims=True) * (inverse * inverse / width)
    slope_high = slope.astype(jnp.bfloat16).astype(jnp.float32)
    lane = lax.broadcasted_iota(jnp.int32, (rows, WIDE), 1)
    second = jnp.where(lane == WIDE - 2, slope_high, activation)
    second = jnp.where(lane == WIDE - 1, slope - slope_high, second)
    zeros8 = jnp.zeros((8, LANES), jnp.float32)
    tail = jnp.concatenate([codes, zeros8, zeros8, zeros8], axis=1)
    body = jnp.concatenate([back_pre * inverse, second], axis=1)
    factors[me] = jnp.concatenate([body, tail], axis=0).astype(jnp.bfloat16)

    @pl.when(has_right)
    def _():
        factor_along(me, 1).start()

    @pl.when(has_left)
    def _():
        factor_along(me, -1).start()

    def arrivals(distance, j):
        for step in (1, -1):
            origin = me - step * distance
            there = (origin >= 0) if step > 0 else (origin < n)
            on = has_right if step > 0 else has_left

            @pl.when(there)
            def _(origin=origin, step=step, on=on):
                for kind in (0, 1):
                    along(origin, kind, j, step).wait_recv()

                    @pl.when(on)
                    def _(kind=kind):
                        along(origin, kind, j, step).start()

    def factor_arrivals(distance):
        for step in (1, -1):
            origin = me - step * distance
            there = (origin >= 0) if step > 0 else (origin < n)
            on = has_right if step > 0 else has_left

            @pl.when(there)
            def _(origin=origin, step=step, on=on):
                factor_along(origin, step).wait_recv()

                @pl.when(on)
                def _():
                    factor_along(origin, step).start()

    for distance in range(1, n - 1):
        for j in range(parts):
            arrivals(distance, j)
        factor_arrivals(distance)
    factor_arrivals(n - 1)

    want_copy().wait()
    body_all = jnp.concatenate(
        [factors[a, :, :].astype(jnp.float32)[:rows] for a in range(n)], axis=0
    )
    body_b = body_all.astype(jnp.bfloat16)
    codes_all = factors[0, :, :].astype(jnp.float32)[rows : rows + 1, : n * rows]
    for a in range(1, n):
        codes_all += factors[a, :, :].astype(jnp.float32)[rows : rows + 1, : n * rows]
    mine = (me + 1).astype(jnp.float32)
    select = jnp.where(codes_all == mine, wanted[...][:, : n * rows], 0.0).astype(jnp.bfloat16)
    chosen = jnp.dot(select, body_b, preferred_element_type=jnp.float32)
    chosen_back = chosen[:, :WIDE].astype(jnp.bfloat16)
    chosen_slope = jnp.sum(
        jnp.where(lane >= WIDE - 2, chosen[:, WIDE:], 0.0), axis=-1, keepdims=True
    )
    weights_t = jnp.transpose(body_all)
    down_t = weights_t[:rank].astype(jnp.bfloat16)
    up_t = weights_t[WIDE : WIDE + rank].astype(jnp.bfloat16)

    def finish(j, carry):
        arrivals(n - 1, j)
        gain = gain_ref[:, cols(j)]

        def whole(kind):
            blocks = [rows_all[a, kind, :, cols(j)].astype(jnp.float32) for a in range(n)]
            return jnp.concatenate(blocks, axis=0).astype(jnp.bfloat16)

        stash_all, back_all = whole(0), whole(1)
        through = jnp.dot(chosen_back, w_down[:, cols(j)], preferred_element_type=jnp.float32)
        chosen_in = jnp.dot(select, back_all, preferred_element_type=jnp.float32)
        chosen_stash = jnp.dot(select, stash_all, preferred_element_type=jnp.float32)
        out = chosen_in + through * gain - chosen_slope * chosen_stash
        picked[:, cols(j)] = out.astype(jnp.bfloat16)
        back_copy(j).start()
        sum_down = jnp.dot(down_t, stash_all, preferred_element_type=jnp.float32)
        grad_down[:, cols(j)] = (sum_down * (gain / n)).astype(jnp.bfloat16)
        sum_up = jnp.dot(up_t, back_all, preferred_element_type=jnp.float32)
        grad_up[:, cols(j)] = (sum_up / n).astype(jnp.bfloat16)
        return carry

    lax.fori_loop(0, parts, finish, 0)

    def drain(j, carry):
        back_copy(j).wait()
        for kind in (0, 1):

            @pl.when(has_right)
            def _(kind=kind):
                along(me, kind, j, 1, True).wait_send()

            @pl.when(has_left)
            def _(kind=kind):
                along(me, kind, j, -1, True).wait_send()

        for distance in range(1, n):
            for step in (1, -1):
                origin = me - step * distance
                there = (origin >= 0) if step > 0 else (origin < n)
                on = has_right if step > 0 else has_left

                @pl.when(there & on)
                def _(origin=origin, step=step):
                    for kind in (0, 1):
                        along(origin, kind, j, step).wait_send()

        return carry

    lax.fori_loop(0, parts, drain, 0)

    for distance in range(n):
        for step in (1, -1):
            if distance == 0 or distance < n - 1:
                origin = me - step * distance
                there = (origin >= 0) if step > 0 else (origin < n)
                on = has_right if step > 0 else has_left

                @pl.when(there & on)
                def _(origin=origin, step=step):
                    factor_along(origin, step).wait_send()


def gathered(stash, back_in, down_proj, up_proj, gain, sent_to, sent_count, recv_from, back_live):
    sections, n = lax.axis_size("section"), lax.axis_size("peer")
    slots, micro, width = stash.shape[2:]
    rows = slots * micro
    rank = down_proj.shape[1]
    parts = 4
    hbm = pl.BlockSpec(memory_space=pl.ANY)
    vmem = pl.BlockSpec(memory_space=pltpu.VMEM)
    smem = pl.BlockSpec(memory_space=pltpu.SMEM)
    dma = pltpu.SemaphoreType.DMA
    returned, grad_down, grad_up = pl.pallas_call(
        functools.partial(gather_kernel, sections, n, parts),
        out_shape=(
            jax.ShapeDtypeStruct((rows, width), jnp.bfloat16),
            jax.ShapeDtypeStruct((rank, width), jnp.bfloat16),
            jax.ShapeDtypeStruct((rank, width), jnp.bfloat16),
        ),
        in_specs=[hbm, hbm, hbm, hbm, vmem, smem, smem, smem, smem],
        out_specs=(vmem, vmem, vmem),
        scratch_shapes=[
            pltpu.VMEM((n, 2, rows, width), jnp.bfloat16),
            pltpu.VMEM((n, rows + 8, 2 * WIDE), jnp.bfloat16),
            pltpu.VMEM((WIDE, width), jnp.bfloat16),
            pltpu.VMEM((WIDE, width), jnp.bfloat16),
            pltpu.VMEM((rows, LANES), jnp.float32),
            pltpu.VMEM((rows, LANES), jnp.float32),
            pltpu.VMEM((rows, width), jnp.bfloat16),
            dma((4,)),
            dma((n, 2, parts)),
            dma((n, 2, parts)),
            dma((n, 2, parts)),
            dma((n,)),
            dma((n,)),
            dma((n,)),
            dma((2,)),
            dma((parts,)),
            dma((parts,)),
        ],
        compiler_params=pltpu.CompilerParams(
            collective_id=0, has_side_effects=True, vmem_limit_bytes=40 * 1024 * 1024
        ),
        cost_estimate=pl.CostEstimate(
            flops=10 * n * rows * rank * width, bytes_accessed=16 * rank * width, transcendentals=0
        ),
    )(
        stash.reshape(rows, width),
        back_in.reshape(rows, width),
        down_proj[0],
        up_proj[0],
        gain,
        sent_to,
        sent_count,
        recv_from,
        back_live,
    )
    return returned.reshape(stash.shape), grad_down[None], grad_up[None]


def by_size(stash, *rest):
    n, sections = lax.axis_size("peer"), lax.axis_size("section")
    rows = stash.shape[2] * stash.shape[3]
    few = n * rows <= LANES and n > 2 and sections > 2
    return (gathered if few else on_device)(stash, *rest)


def solution(mesh):
    placed = (
        P("section", "peer", None, None, None),
        P("section", "peer", None, None, None),
        P("section", None, None),
        P("section", None, None),
        P("section", None),
        P("section", "peer", None),
        P("section", "peer"),
        P("section", "peer", None),
        P("section", "peer", None),
    )
    return jax.shard_map(
        by_size,
        mesh=mesh,
        in_specs=placed,
        out_specs=(
            P("section", "peer", None, None, None),
            P("section", None, None),
            P("section", None, None),
        ),
        check_vma=False,
    )
```

```python
import functools

import jax
import jax.numpy as jnp
from jax import lax
from jax.experimental import pallas as pl
from jax.experimental.pallas import tpu as pltpu
from jax.sharding import PartitionSpec as P

MESH = pl.DeviceIdType.MESH
LANES = 128
WIDE = 256

epsilon = 1e-05


def passed_along(block, axis, distance):
    devices = range(lax.axis_size(axis))
    route = [((i - distance) % len(devices), i) for i in devices]
    return lax.ppermute(block, axis, route)


def compact(blocks, targets, live_count):
    peer_count = blocks.shape[0]
    send_slots = targets.shape[0]
    peer_index = jnp.arange(peer_count, dtype=jnp.int32)
    slot_index = jnp.arange(send_slots, dtype=jnp.int32)
    selector = (
        (targets[:, None] == peer_index[None, :]) & (slot_index[:, None] < live_count)
    ).astype(jnp.bfloat16)
    flat = blocks.reshape(peer_count, -1)
    packed = jnp.dot(selector, flat, preferred_element_type=jnp.float32).astype(jnp.bfloat16)
    return packed.reshape((send_slots,) + blocks.shape[1:])


def on_device(stash, back_in, down_proj, up_proj, gain, sent_to, sent_count, recv_from, back_live):
    peer_count = lax.axis_size("peer")
    live_slots = back_live[0, 0]
    slot_mask = live_slots.astype(jnp.bfloat16)[:, None, None]
    slot_count = stash.shape[2]
    micro_rows = stash.shape[3]
    model_width = stash.shape[4]
    stored = (stash[0, 0] * slot_mask).reshape(slot_count * micro_rows, model_width)
    incoming = (back_in[0, 0] * slot_mask).reshape(slot_count * micro_rows, model_width)
    section_gain = gain[0]
    down_local = down_proj[0]
    up_local = up_proj[0]
    stored_f = stored.astype(jnp.float32)
    inverse = lax.rsqrt(jnp.mean(stored_f * stored_f, axis=-1, keepdims=True) + epsilon)
    unit_rows = stored_f * inverse
    normed = (unit_rows * section_gain).astype(jnp.bfloat16)
    contract_last = (((1,), (1,)), ((), ()))
    contract_rows = (((0,), (0,)), ((), ()))
    preact = lax.dot_general(normed, down_local, contract_last, preferred_element_type=jnp.float32)
    sigmoid_pre = jax.nn.sigmoid(preact)
    activation = (preact * sigmoid_pre).astype(jnp.bfloat16)
    back_act = lax.dot_general(
        incoming, up_local, contract_last, preferred_element_type=jnp.float32
    )
    back_pre = (back_act * (sigmoid_pre * (1.0 + preact * (1.0 - sigmoid_pre)))).astype(
        jnp.bfloat16
    )
    back_norm = jnp.dot(back_pre, down_local, preferred_element_type=jnp.float32) * section_gain
    input_grad = incoming.astype(jnp.float32) + inverse * (
        back_norm - unit_rows * jnp.mean(back_norm * unit_rows, axis=-1, keepdims=True)
    )
    input_grad = input_grad.astype(jnp.bfloat16)
    peer_index = jnp.arange(peer_count, dtype=jnp.int32)
    spreader = (
        (recv_from[0, 0][None, :] == peer_index[:, None]) & (live_slots[None, :] == 1)
    ).astype(jnp.bfloat16)
    by_sender = jnp.dot(
        spreader, input_grad.reshape(slot_count, -1), preferred_element_type=jnp.float32
    ).astype(jnp.bfloat16)
    by_sender = by_sender.reshape(peer_count, micro_rows, model_width)
    exchanged = lax.all_to_all(by_sender, "peer", split_axis=0, concat_axis=0, tiled=True)
    arrived = passed_along(exchanged, "section", -1)
    returned = compact(arrived, sent_to[0, 0], sent_count[0, 0])
    part_down = (
        lax.dot_general(back_pre, normed, contract_rows, preferred_element_type=jnp.float32)
        .astype(jnp.bfloat16)
        .astype(jnp.float32)
    )
    part_up = (
        lax.dot_general(activation, incoming, contract_rows, preferred_element_type=jnp.float32)
        .astype(jnp.bfloat16)
        .astype(jnp.float32)
    )
    summed_down, summed_up = (
        lax.psum(part_down.astype(jnp.bfloat16), "peer").astype(jnp.float32),
        lax.psum(part_up.astype(jnp.bfloat16), "peer").astype(jnp.float32),
    )
    grad_down = (summed_down / peer_count).astype(jnp.bfloat16)
    grad_up = (summed_up / peer_count).astype(jnp.bfloat16)
    return (returned[None, None], grad_down[None], grad_up[None])


def gather_kernel(
    sections,
    n,
    parts,
    stash,
    back_in,
    down,
    up,
    gain_in,
    sent_to_in,
    sent_count_in,
    recv_from_in,
    back_live_in,
    returned,
    grad_down_out,
    grad_up_out,
    rows_all,
    factors,
    w_down,
    w_up,
    asked,
    wanted,
    picked,
    grad_down,
    grad_up,
    gain_ref,
    sent_to,
    sent_count,
    recv_from,
    back_live,
    local_sem,
    right_sem,
    left_sem,
    recv_sem,
    fac_right,
    fac_left,
    fac_recv,
    want_sem,
    back_send,
    back_recv,
    out_sem,
):
    section = lax.axis_index("section")
    me = lax.axis_index("peer")
    before = lax.rem(section + sections - 1, sections)
    after = lax.rem(section + 1, sections)
    rows, width = stash.shape
    rank = down.shape[0]
    part = width // parts
    has_left, has_right = me > 0, me < n - 1

    def cols(j):
        return pl.ds(pl.multiple_of(j * part, part), part)

    def along(origin, kind, j, step, own=False):
        view = rows_all.at[origin, kind, :, cols(j)]
        source = (stash, back_in)[kind].at[:, cols(j)] if own else view
        return pltpu.make_async_remote_copy(
            src_ref=source,
            dst_ref=view,
            send_sem=(right_sem if step > 0 else left_sem).at[origin, kind, j],
            recv_sem=recv_sem.at[origin, kind, j],
            device_id=(section, me + step),
            device_id_type=MESH,
        )

    def factor_along(origin, step):
        return pltpu.make_async_remote_copy(
            src_ref=factors.at[origin],
            dst_ref=factors.at[origin],
            send_sem=(fac_right if step > 0 else fac_left).at[origin],
            recv_sem=fac_recv.at[origin],
            device_id=(section, me + step),
            device_id_type=MESH,
        )

    def want_copy():
        return pltpu.make_async_remote_copy(
            src_ref=asked,
            dst_ref=wanted,
            send_sem=want_sem.at[0],
            recv_sem=want_sem.at[1],
            device_id=(after, me),
            device_id_type=MESH,
        )

    def back_copy(j):
        return pltpu.make_async_remote_copy(
            src_ref=picked.at[:, cols(j)],
            dst_ref=returned.at[:, cols(j)],
            send_sem=back_send.at[j],
            recv_sem=back_recv.at[j],
            device_id=(before, me),
            device_id_type=MESH,
        )

    small = [
        pltpu.make_async_copy(sent_to_in, sent_to, local_sem.at[5]),
        pltpu.make_async_copy(sent_count_in, sent_count, local_sem.at[6]),
        pltpu.make_async_copy(recv_from_in, recv_from, local_sem.at[7]),
        pltpu.make_async_copy(back_live_in, back_live, local_sem.at[8]),
    ]
    def stores(j):
        return (
            pltpu.make_async_copy(
                grad_down.at[:, cols(j)], grad_down_out.at[:, cols(j)], out_sem.at[0, j]
            ),
            pltpu.make_async_copy(
                grad_up.at[:, cols(j)], grad_up_out.at[:, cols(j)], out_sem.at[1, j]
            ),
        )

    loads = [
        pltpu.make_async_copy(stash, rows_all.at[me, 0], local_sem.at[0]),
        pltpu.make_async_copy(back_in, rows_all.at[me, 1], local_sem.at[1]),
        pltpu.make_async_copy(down, w_down.at[pl.ds(0, rank)], local_sem.at[2]),
        pltpu.make_async_copy(up, w_up.at[pl.ds(0, rank)], local_sem.at[3]),
        pltpu.make_async_copy(gain_in, gain_ref, local_sem.at[4]),
    ]
    for load in small + loads:
        load.start()

    barrier = pltpu.get_barrier_semaphore()
    for other in (before, after):
        pl.semaphore_signal(barrier, inc=1, device_id=(other, me), device_id_type=MESH)

    @pl.when(has_left)
    def _():
        pl.semaphore_signal(barrier, inc=1, device_id=(section, me - 1), device_id_type=MESH)

    @pl.when(has_right)
    def _():
        pl.semaphore_signal(barrier, inc=1, device_id=(section, me + 1), device_id_type=MESH)

    @pl.when(has_left & has_right)
    def _():
        pl.semaphore_wait(barrier, 4)

    @pl.when(jnp.logical_not(has_left & has_right))
    def _():
        pl.semaphore_wait(barrier, 3)

    for j in range(parts):
        for kind in (0, 1):

            @pl.when(has_right)
            def _(j=j, kind=kind):
                along(me, kind, j, 1, True).start()

            @pl.when(has_left)
            def _(j=j, kind=kind):
                along(me, kind, j, -1, True).start()

    for load in small:
        load.wait()
    slots = sent_to.shape[2]
    micro = rows // slots
    at_row = lax.broadcasted_iota(jnp.int32, (rows, LANES), 0)
    at_lane = lax.broadcasted_iota(jnp.int32, (rows, LANES), 1)
    lane_peer = jnp.zeros((rows, LANES), jnp.int32)
    for a in range(1, n):
        lane_peer += jnp.where(at_lane >= a * rows, 1, 0)
    target = jnp.full((rows, LANES), -1, jnp.int32)
    for k in range(slots):
        here = (at_row >= k * micro) & (at_row < (k + 1) * micro)
        target = jnp.where(here & (sent_count[0, 0] > k), sent_to[0, 0, k], target)
    same = lax.rem(at_lane, micro) == lax.rem(at_row, micro)
    asked[...] = jnp.where(same & (lane_peer == target), 1.0, 0.0)
    want_copy().start()

    w_down[pl.ds(rank, WIDE - rank), :] = jnp.zeros((WIDE - rank, width), jnp.bfloat16)
    w_up[pl.ds(rank, WIDE - rank), :] = jnp.zeros((WIDE - rank, width), jnp.bfloat16)
    for load in loads:
        load.wait()

    def square_part(j, total):
        block = rows_all[me, 0, :, cols(j)].astype(jnp.float32)
        return total + jnp.sum(block * block, axis=-1, keepdims=True)

    squares = lax.fori_loop(0, parts, square_part, jnp.zeros((rows, 1), jnp.float32))
    inverse = lax.rsqrt(squares / width + epsilon)
    contract_last = (((1,), (1,)), ((), ()))

    def project_part(j, carry):
        pre, back = carry
        block = rows_all[me, 0, :, cols(j)].astype(jnp.float32)
        normed = (block * inverse * gain_ref[:, cols(j)]).astype(jnp.bfloat16)
        pre = pre + lax.dot_general(
            normed, w_down[:, cols(j)], contract_last, preferred_element_type=jnp.float32
        )
        back = back + lax.dot_general(
            rows_all[me, 1, :, cols(j)],
            w_up[:, cols(j)],
            contract_last,
            preferred_element_type=jnp.float32,
        )
        return pre, back

    empty = jnp.zeros((rows, WIDE), jnp.float32)
    preact, back_act = lax.fori_loop(0, parts, project_part, (empty, empty))
    row_only = lax.broadcasted_iota(jnp.int32, (rows, 1), 0)
    code_lane = lax.broadcasted_iota(jnp.int32, (8, LANES), 1) - me * rows
    live = jnp.zeros((rows, 1), jnp.float32)
    codes = jnp.zeros((8, LANES), jnp.float32)
    for k in range(slots):
        held = back_live[0, 0, k]
        here = (row_only >= k * micro) & (row_only < (k + 1) * micro)
        live = jnp.where(here, held.astype(jnp.float32), live)
        here = (code_lane >= k * micro) & (code_lane < (k + 1) * micro)
        codes = jnp.where(here, ((recv_from[0, 0, k] + 1) * held).astype(jnp.float32), codes)
    sigmoid_pre = jax.nn.sigmoid(preact)
    activation = preact * sigmoid_pre * live
    back_pre = back_act * (sigmoid_pre * (1.0 + preact * (1.0 - sigmoid_pre))) * live
    slope = jnp.sum(back_pre * preact, axis=-1, keepdims=True) * (inverse * inverse / width)
    slope_high = slope.astype(jnp.bfloat16).astype(jnp.float32)
    lane = lax.broadcasted_iota(jnp.int32, (rows, WIDE), 1)
    second = jnp.where(lane == WIDE - 2, slope_high, activation)
    second = jnp.where(lane == WIDE - 1, slope - slope_high, second)
    zeros8 = jnp.zeros((8, LANES), jnp.float32)
    tail = jnp.concatenate([codes, zeros8, zeros8, zeros8], axis=1)
    body = jnp.concatenate([back_pre * inverse, second], axis=1)
    factors[me] = jnp.concatenate([body, tail], axis=0).astype(jnp.bfloat16)

    @pl.when(has_right)
    def _():
        factor_along(me, 1).start()

    @pl.when(has_left)
    def _():
        factor_along(me, -1).start()

    def arrivals(distance, j):
        for step in (1, -1):
            origin = me - step * distance
            there = (origin >= 0) if step > 0 else (origin < n)
            on = has_right if step > 0 else has_left

            @pl.when(there)
            def _(origin=origin, step=step, on=on):
                for kind in (0, 1):
                    along(origin, kind, j, step).wait_recv()

                    @pl.when(on)
                    def _(kind=kind):
                        along(origin, kind, j, step).start()

    def factor_arrivals(distance):
        for step in (1, -1):
            origin = me - step * distance
            there = (origin >= 0) if step > 0 else (origin < n)
            on = has_right if step > 0 else has_left

            @pl.when(there)
            def _(origin=origin, step=step, on=on):
                factor_along(origin, step).wait_recv()

                @pl.when(on)
                def _():
                    factor_along(origin, step).start()

    for distance in range(1, n):
        arrivals(distance, 0)
        factor_arrivals(distance)
        if distance < n - 1:
            for j in range(1, parts):
                arrivals(distance, j)

    want_copy().wait()
    body_all = jnp.concatenate(
        [factors[a, :, :].astype(jnp.float32)[:rows] for a in range(n)], axis=0
    )
    body_b = body_all.astype(jnp.bfloat16)
    codes_all = factors[0, :, :].astype(jnp.float32)[rows : rows + 1, : n * rows]
    for a in range(1, n):
        codes_all += factors[a, :, :].astype(jnp.float32)[rows : rows + 1, : n * rows]
    mine = (me + 1).astype(jnp.float32)
    select = jnp.where(codes_all == mine, wanted[...][:, : n * rows], 0.0).astype(jnp.bfloat16)
    chosen = jnp.dot(select, body_b, preferred_element_type=jnp.float32)
    chosen_back = chosen[:, :WIDE].astype(jnp.bfloat16)
    chosen_slope = jnp.sum(
        jnp.where(lane >= WIDE - 2, chosen[:, WIDE:], 0.0), axis=-1, keepdims=True
    )
    weights_t = jnp.transpose(body_all)
    down_t = weights_t[:rank].astype(jnp.bfloat16)
    up_t = weights_t[WIDE : WIDE + rank].astype(jnp.bfloat16)

    def finish(j, carry):
        @pl.when(j > 0)
        def _():
            arrivals(n - 1, j)

        gain = gain_ref[:, cols(j)]

        def whole(kind):
            blocks = [rows_all[a, kind, :, cols(j)].astype(jnp.float32) for a in range(n)]
            return jnp.concatenate(blocks, axis=0).astype(jnp.bfloat16)

        stash_all, back_all = whole(0), whole(1)
        through = jnp.dot(chosen_back, w_down[:, cols(j)], preferred_element_type=jnp.float32)
        chosen_in = jnp.dot(select, back_all, preferred_element_type=jnp.float32)
        chosen_stash = jnp.dot(select, stash_all, preferred_element_type=jnp.float32)
        out = chosen_in + through * gain - chosen_slope * chosen_stash
        picked[:, cols(j)] = out.astype(jnp.bfloat16)
        back_copy(j).start()
        sum_down = jnp.dot(down_t, stash_all, preferred_element_type=jnp.float32)
        grad_down[:, cols(j)] = (sum_down * (gain / n)).astype(jnp.bfloat16)
        sum_up = jnp.dot(up_t, back_all, preferred_element_type=jnp.float32)
        grad_up[:, cols(j)] = (sum_up / n).astype(jnp.bfloat16)
        for store in stores(j):
            store.start()
        return carry

    lax.fori_loop(0, parts, finish, 0)

    def drain(j, carry):
        back_copy(j).wait()
        for store in stores(j):
            store.wait()
        for kind in (0, 1):

            @pl.when(has_right)
            def _(kind=kind):
                along(me, kind, j, 1, True).wait_send()

            @pl.when(has_left)
            def _(kind=kind):
                along(me, kind, j, -1, True).wait_send()

        for distance in range(1, n):
            for step in (1, -1):
                origin = me - step * distance
                there = (origin >= 0) if step > 0 else (origin < n)
                on = has_right if step > 0 else has_left

                @pl.when(there & on)
                def _(origin=origin, step=step):
                    for kind in (0, 1):
                        along(origin, kind, j, step).wait_send()

        return carry

    lax.fori_loop(0, parts, drain, 0)

    for distance in range(n):
        for step in (1, -1):
            if distance == 0 or distance < n - 1:
                origin = me - step * distance
                there = (origin >= 0) if step > 0 else (origin < n)
                on = has_right if step > 0 else has_left

                @pl.when(there & on)
                def _(origin=origin, step=step):
                    factor_along(origin, step).wait_send()


def gathered(stash, back_in, down_proj, up_proj, gain, sent_to, sent_count, recv_from, back_live):
    sections, n = lax.axis_size("section"), lax.axis_size("peer")
    slots, micro, width = stash.shape[2:]
    rows = slots * micro
    rank = down_proj.shape[1]
    parts = 4
    hbm = pl.BlockSpec(memory_space=pltpu.HBM)
    dma = pltpu.SemaphoreType.DMA
    returned, grad_down, grad_up = pl.pallas_call(
        functools.partial(gather_kernel, sections, n, parts),
        out_shape=(
            jax.ShapeDtypeStruct((rows, width), jnp.bfloat16),
            jax.ShapeDtypeStruct((rank, width), jnp.bfloat16),
            jax.ShapeDtypeStruct((rank, width), jnp.bfloat16),
        ),
        in_specs=[hbm] * 9,
        out_specs=(hbm, hbm, hbm),
        scratch_shapes=[
            pltpu.VMEM((n, 2, rows, width), jnp.bfloat16),
            pltpu.VMEM((n, rows + 8, 2 * WIDE), jnp.bfloat16),
            pltpu.VMEM((WIDE, width), jnp.bfloat16),
            pltpu.VMEM((WIDE, width), jnp.bfloat16),
            pltpu.VMEM((rows, LANES), jnp.float32),
            pltpu.VMEM((rows, LANES), jnp.float32),
            pltpu.VMEM((rows, width), jnp.bfloat16),
            pltpu.VMEM((rank, width), jnp.bfloat16),
            pltpu.VMEM((rank, width), jnp.bfloat16),
            pltpu.VMEM((1, width), jnp.float32),
            pltpu.SMEM(sent_to.shape, jnp.int32),
            pltpu.SMEM(sent_count.shape, jnp.int32),
            pltpu.SMEM(recv_from.shape, jnp.int32),
            pltpu.SMEM(back_live.shape, jnp.int32),
            dma((9,)),
            dma((n, 2, parts)),
            dma((n, 2, parts)),
            dma((n, 2, parts)),
            dma((n,)),
            dma((n,)),
            dma((n,)),
            dma((2,)),
            dma((parts,)),
            dma((parts,)),
            dma((2, parts)),
        ],
        compiler_params=pltpu.CompilerParams(
            collective_id=0, has_side_effects=True, vmem_limit_bytes=60 * 1024 * 1024
        ),
        cost_estimate=pl.CostEstimate(
            flops=10 * n * rows * rank * width, bytes_accessed=16 * rank * width, transcendentals=0
        ),
    )(
        stash.reshape(rows, width),
        back_in.reshape(rows, width),
        down_proj[0],
        up_proj[0],
        gain,
        sent_to,
        sent_count,
        recv_from,
        back_live,
    )
    return returned.reshape(stash.shape), grad_down[None], grad_up[None]


def by_size(stash, *rest):
    n, sections = lax.axis_size("peer"), lax.axis_size("section")
    rows = stash.shape[2] * stash.shape[3]
    few = n * rows <= LANES and n > 2 and sections > 2
    return (gathered if few else on_device)(stash, *rest)


def solution(mesh):
    placed = (
        P("section", "peer", None, None, None),
        P("section", "peer", None, None, None),
        P("section", None, None),
        P("section", None, None),
        P("section", None),
        P("section", "peer", None),
        P("section", "peer"),
        P("section", "peer", None),
        P("section", "peer", None),
    )
    return jax.shard_map(
        by_size,
        mesh=mesh,
        in_specs=placed,
        out_specs=(
            P("section", "peer", None, None, None),
            P("section", None, None),
            P("section", None, None),
        ),
        check_vma=False,
    )
```

```python
import functools

import jax
import jax.numpy as jnp
from jax import lax
from jax.experimental import pallas as pl
from jax.experimental.pallas import tpu as pltpu
from jax.sharding import PartitionSpec as P

MESH = pl.DeviceIdType.MESH
LANES = 128
WIDE = 256

epsilon = 1e-05


def passed_along(block, axis, distance):
    devices = range(lax.axis_size(axis))
    route = [((i - distance) % len(devices), i) for i in devices]
    return lax.ppermute(block, axis, route)


def compact(blocks, targets, live_count):
    peer_count = blocks.shape[0]
    send_slots = targets.shape[0]
    peer_index = jnp.arange(peer_count, dtype=jnp.int32)
    slot_index = jnp.arange(send_slots, dtype=jnp.int32)
    selector = (
        (targets[:, None] == peer_index[None, :]) & (slot_index[:, None] < live_count)
    ).astype(jnp.bfloat16)
    flat = blocks.reshape(peer_count, -1)
    packed = jnp.dot(selector, flat, preferred_element_type=jnp.float32).astype(jnp.bfloat16)
    return packed.reshape((send_slots,) + blocks.shape[1:])


def on_device(stash, back_in, down_proj, up_proj, gain, sent_to, sent_count, recv_from, back_live):
    peer_count = lax.axis_size("peer")
    live_slots = back_live[0, 0]
    slot_mask = live_slots.astype(jnp.bfloat16)[:, None, None]
    slot_count = stash.shape[2]
    micro_rows = stash.shape[3]
    model_width = stash.shape[4]
    stored = (stash[0, 0] * slot_mask).reshape(slot_count * micro_rows, model_width)
    incoming = (back_in[0, 0] * slot_mask).reshape(slot_count * micro_rows, model_width)
    section_gain = gain[0]
    down_local = down_proj[0]
    up_local = up_proj[0]
    stored_f = stored.astype(jnp.float32)
    inverse = lax.rsqrt(jnp.mean(stored_f * stored_f, axis=-1, keepdims=True) + epsilon)
    unit_rows = stored_f * inverse
    normed = (unit_rows * section_gain).astype(jnp.bfloat16)
    contract_last = (((1,), (1,)), ((), ()))
    contract_rows = (((0,), (0,)), ((), ()))
    preact = lax.dot_general(normed, down_local, contract_last, preferred_element_type=jnp.float32)
    sigmoid_pre = jax.nn.sigmoid(preact)
    activation = (preact * sigmoid_pre).astype(jnp.bfloat16)
    back_act = lax.dot_general(
        incoming, up_local, contract_last, preferred_element_type=jnp.float32
    )
    back_pre = (back_act * (sigmoid_pre * (1.0 + preact * (1.0 - sigmoid_pre)))).astype(
        jnp.bfloat16
    )
    back_norm = jnp.dot(back_pre, down_local, preferred_element_type=jnp.float32) * section_gain
    input_grad = incoming.astype(jnp.float32) + inverse * (
        back_norm - unit_rows * jnp.mean(back_norm * unit_rows, axis=-1, keepdims=True)
    )
    input_grad = input_grad.astype(jnp.bfloat16)
    peer_index = jnp.arange(peer_count, dtype=jnp.int32)
    spreader = (
        (recv_from[0, 0][None, :] == peer_index[:, None]) & (live_slots[None, :] == 1)
    ).astype(jnp.bfloat16)
    by_sender = jnp.dot(
        spreader, input_grad.reshape(slot_count, -1), preferred_element_type=jnp.float32
    ).astype(jnp.bfloat16)
    by_sender = by_sender.reshape(peer_count, micro_rows, model_width)
    exchanged = lax.all_to_all(by_sender, "peer", split_axis=0, concat_axis=0, tiled=True)
    arrived = passed_along(exchanged, "section", -1)
    returned = compact(arrived, sent_to[0, 0], sent_count[0, 0])
    part_down = (
        lax.dot_general(back_pre, normed, contract_rows, preferred_element_type=jnp.float32)
        .astype(jnp.bfloat16)
        .astype(jnp.float32)
    )
    part_up = (
        lax.dot_general(activation, incoming, contract_rows, preferred_element_type=jnp.float32)
        .astype(jnp.bfloat16)
        .astype(jnp.float32)
    )
    summed_down, summed_up = (
        lax.psum(part_down.astype(jnp.bfloat16), "peer").astype(jnp.float32),
        lax.psum(part_up.astype(jnp.bfloat16), "peer").astype(jnp.float32),
    )
    grad_down = (summed_down / peer_count).astype(jnp.bfloat16)
    grad_up = (summed_up / peer_count).astype(jnp.bfloat16)
    return (returned[None, None], grad_down[None], grad_up[None])


def gather_kernel(
    sections,
    n,
    parts,
    stash,
    back_in,
    down,
    up,
    gain_in,
    sent_to_in,
    sent_count_in,
    recv_from_in,
    back_live_in,
    returned,
    grad_down_out,
    grad_up_out,
    rows_all,
    factors,
    w_down,
    w_up,
    asked,
    wanted,
    picked,
    grad_down,
    grad_up,
    gain_ref,
    sent_to,
    sent_count,
    recv_from,
    back_live,
    local_sem,
    right_sem,
    left_sem,
    recv_sem,
    fac_right,
    fac_left,
    fac_recv,
    want_sem,
    back_send,
    back_recv,
    out_sem,
):
    section = lax.axis_index("section")
    me = lax.axis_index("peer")
    before = lax.rem(section + sections - 1, sections)
    after = lax.rem(section + 1, sections)
    rows, width = stash.shape
    rank = down.shape[0]
    part = width // parts
    has_left, has_right = me > 0, me < n - 1

    def cols(j):
        return pl.ds(pl.multiple_of(j * part, part), part)

    def along(origin, kind, j, step, own=False):
        view = rows_all.at[origin, kind, :, cols(j)]
        source = (stash, back_in)[kind].at[:, cols(j)] if own else view
        return pltpu.make_async_remote_copy(
            src_ref=source,
            dst_ref=view,
            send_sem=(right_sem if step > 0 else left_sem).at[origin, kind, j],
            recv_sem=recv_sem.at[origin, kind, j],
            device_id=(section, me + step),
            device_id_type=MESH,
        )

    def factor_along(origin, step):
        return pltpu.make_async_remote_copy(
            src_ref=factors.at[origin],
            dst_ref=factors.at[origin],
            send_sem=(fac_right if step > 0 else fac_left).at[origin],
            recv_sem=fac_recv.at[origin],
            device_id=(section, me + step),
            device_id_type=MESH,
        )

    def want_copy():
        return pltpu.make_async_remote_copy(
            src_ref=asked,
            dst_ref=wanted,
            send_sem=want_sem.at[0],
            recv_sem=want_sem.at[1],
            device_id=(after, me),
            device_id_type=MESH,
        )

    def back_copy(j):
        return pltpu.make_async_remote_copy(
            src_ref=picked.at[:, cols(j)],
            dst_ref=returned.at[:, cols(j)],
            send_sem=back_send.at[j],
            recv_sem=back_recv.at[j],
            device_id=(before, me),
            device_id_type=MESH,
        )

    small = [
        pltpu.make_async_copy(sent_to_in, sent_to, local_sem.at[5]),
        pltpu.make_async_copy(sent_count_in, sent_count, local_sem.at[6]),
        pltpu.make_async_copy(recv_from_in, recv_from, local_sem.at[7]),
        pltpu.make_async_copy(back_live_in, back_live, local_sem.at[8]),
    ]
    def stores(j):
        return (
            pltpu.make_async_copy(
                grad_down.at[:, cols(j)], grad_down_out.at[:, cols(j)], out_sem.at[0, j]
            ),
            pltpu.make_async_copy(
                grad_up.at[:, cols(j)], grad_up_out.at[:, cols(j)], out_sem.at[1, j]
            ),
        )

    loads = [
        pltpu.make_async_copy(stash, rows_all.at[me, 0], local_sem.at[0]),
        pltpu.make_async_copy(back_in, rows_all.at[me, 1], local_sem.at[1]),
        pltpu.make_async_copy(down, w_down.at[pl.ds(0, rank)], local_sem.at[2]),
        pltpu.make_async_copy(up, w_up.at[pl.ds(0, rank)], local_sem.at[3]),
        pltpu.make_async_copy(gain_in, gain_ref, local_sem.at[4]),
    ]
    for load in small + loads:
        load.start()

    barrier = pltpu.get_barrier_semaphore()
    for other in (before, after):
        pl.semaphore_signal(barrier, inc=1, device_id=(other, me), device_id_type=MESH)

    @pl.when(has_left)
    def _():
        pl.semaphore_signal(barrier, inc=1, device_id=(section, me - 1), device_id_type=MESH)

    @pl.when(has_right)
    def _():
        pl.semaphore_signal(barrier, inc=1, device_id=(section, me + 1), device_id_type=MESH)

    @pl.when(has_left & has_right)
    def _():
        pl.semaphore_wait(barrier, 4)

    @pl.when(jnp.logical_not(has_left & has_right))
    def _():
        pl.semaphore_wait(barrier, 3)

    for j in range(parts):
        for kind in (0, 1):

            @pl.when(has_right)
            def _(j=j, kind=kind):
                along(me, kind, j, 1, True).start()

            @pl.when(has_left)
            def _(j=j, kind=kind):
                along(me, kind, j, -1, True).start()

    for load in small:
        load.wait()
    slots = sent_to.shape[2]
    micro = rows // slots
    at_row = lax.broadcasted_iota(jnp.int32, (rows, LANES), 0)
    at_lane = lax.broadcasted_iota(jnp.int32, (rows, LANES), 1)
    lane_peer = jnp.zeros((rows, LANES), jnp.int32)
    for a in range(1, n):
        lane_peer += jnp.where(at_lane >= a * rows, 1, 0)
    target = jnp.full((rows, LANES), -1, jnp.int32)
    for k in range(slots):
        here = (at_row >= k * micro) & (at_row < (k + 1) * micro)
        target = jnp.where(here & (sent_count[0, 0] > k), sent_to[0, 0, k], target)
    same = lax.rem(at_lane, micro) == lax.rem(at_row, micro)
    asked[...] = jnp.where(same & (lane_peer == target), 1.0, 0.0)
    want_copy().start()

    w_down[pl.ds(rank, WIDE - rank), :] = jnp.zeros((WIDE - rank, width), jnp.bfloat16)
    w_up[pl.ds(rank, WIDE - rank), :] = jnp.zeros((WIDE - rank, width), jnp.bfloat16)
    for load in loads:
        load.wait()

    def square_part(j, total):
        block = rows_all[me, 0, :, cols(j)].astype(jnp.float32)
        return total + jnp.sum(block * block, axis=-1, keepdims=True)

    squares = lax.fori_loop(0, parts, square_part, jnp.zeros((rows, 1), jnp.float32))
    inverse = lax.rsqrt(squares / width + epsilon)
    contract_last = (((1,), (1,)), ((), ()))

    def project_part(j, carry):
        pre, back = carry
        block = rows_all[me, 0, :, cols(j)].astype(jnp.float32)
        normed = (block * inverse * gain_ref[:, cols(j)]).astype(jnp.bfloat16)
        pre = pre + lax.dot_general(
            normed, w_down[:, cols(j)], contract_last, preferred_element_type=jnp.float32
        )
        back = back + lax.dot_general(
            rows_all[me, 1, :, cols(j)],
            w_up[:, cols(j)],
            contract_last,
            preferred_element_type=jnp.float32,
        )
        return pre, back

    empty = jnp.zeros((rows, WIDE), jnp.float32)
    preact, back_act = lax.fori_loop(0, parts, project_part, (empty, empty))
    row_only = lax.broadcasted_iota(jnp.int32, (rows, 1), 0)
    live = jnp.zeros((rows, 1), jnp.float32)
    code = jnp.zeros((rows, 1), jnp.float32)
    for k in range(slots):
        held = back_live[0, 0, k]
        here = (row_only >= k * micro) & (row_only < (k + 1) * micro)
        live = jnp.where(here, held.astype(jnp.float32), live)
        code = jnp.where(here, ((recv_from[0, 0, k] + 1) * held).astype(jnp.float32), code)
    sigmoid_pre = jax.nn.sigmoid(preact)
    activation = preact * sigmoid_pre * live
    back_pre = back_act * (sigmoid_pre * (1.0 + preact * (1.0 - sigmoid_pre))) * live
    slope = jnp.sum(back_pre * preact, axis=-1, keepdims=True) * (inverse * inverse / width)
    slope_high = slope.astype(jnp.bfloat16).astype(jnp.float32)
    packed = factors.shape[2]
    extra = jnp.zeros((rows, packed - WIDE), jnp.float32)
    lane = lax.broadcasted_iota(jnp.int32, (rows, packed), 1)
    body = jnp.concatenate([back_pre * inverse, extra], axis=1)
    body += pltpu.roll(jnp.concatenate([activation, extra], axis=1), rank, 1)
    for at, value in enumerate((slope_high, slope - slope_high, code)):
        body = jnp.where(lane == 2 * rank + at, value, body)
    factors[me] = body.astype(jnp.bfloat16)

    @pl.when(has_right)
    def _():
        factor_along(me, 1).start()

    @pl.when(has_left)
    def _():
        factor_along(me, -1).start()

    def arrivals(distance, j):
        for step in (1, -1):
            origin = me - step * distance
            there = (origin >= 0) if step > 0 else (origin < n)
            on = has_right if step > 0 else has_left

            @pl.when(there)
            def _(origin=origin, step=step, on=on):
                for kind in (0, 1):
                    along(origin, kind, j, step).wait_recv()

                    @pl.when(on)
                    def _(kind=kind):
                        along(origin, kind, j, step).start()

    def factor_arrivals(distance):
        for step in (1, -1):
            origin = me - step * distance
            there = (origin >= 0) if step > 0 else (origin < n)
            on = has_right if step > 0 else has_left

            @pl.when(there)
            def _(origin=origin, step=step, on=on):
                factor_along(origin, step).wait_recv()

                @pl.when(on)
                def _():
                    factor_along(origin, step).start()

    for distance in range(1, n):
        arrivals(distance, 0)
        factor_arrivals(distance)
        if distance < n - 1:
            for j in range(1, parts):
                arrivals(distance, j)

    want_copy().wait()
    body_all = jnp.concatenate([factors[a].astype(jnp.float32) for a in range(n)], axis=0)
    body_t = jnp.transpose(body_all)
    mine = (me + 1).astype(jnp.float32)
    codes_all = body_t[2 * rank + 2 : 2 * rank + 3]
    select = jnp.where(codes_all == mine, wanted[...][:, : n * rows], 0.0)
    chosen = jnp.dot(
        select.astype(jnp.bfloat16), body_all.astype(jnp.bfloat16), preferred_element_type=jnp.float32
    )
    chosen_back = chosen[:, :WIDE].astype(jnp.bfloat16)
    slope_lane = (lane == 2 * rank) | (lane == 2 * rank + 1)
    chosen_slope = jnp.sum(jnp.where(slope_lane, chosen, 0.0), axis=-1, keepdims=True)
    down_pick = jnp.concatenate([select, body_t[:rank]], axis=0).astype(jnp.bfloat16)
    up_pick = jnp.concatenate([select, body_t[rank : 2 * rank]], axis=0).astype(jnp.bfloat16)

    def finish(j, carry):
        @pl.when(j > 0)
        def _():
            arrivals(n - 1, j)

        gain = gain_ref[:, cols(j)]

        def whole(kind):
            blocks = [rows_all[a, kind, :, cols(j)].astype(jnp.float32) for a in range(n)]
            return jnp.concatenate(blocks, axis=0).astype(jnp.bfloat16)

        stash_all, back_all = whole(0), whole(1)
        through = jnp.dot(chosen_back, w_down[:, cols(j)], preferred_element_type=jnp.float32)
        from_stash = jnp.dot(down_pick, stash_all, preferred_element_type=jnp.float32)
        from_back = jnp.dot(up_pick, back_all, preferred_element_type=jnp.float32)
        out = from_back[:rows] + through * gain - chosen_slope * from_stash[:rows]
        picked[:, cols(j)] = out.astype(jnp.bfloat16)
        back_copy(j).start()
        grad_down[:, cols(j)] = (from_stash[rows:] * (gain / n)).astype(jnp.bfloat16)
        grad_up[:, cols(j)] = (from_back[rows:] / n).astype(jnp.bfloat16)
        for store in stores(j):
            store.start()
        return carry

    lax.fori_loop(0, parts, finish, 0)

    def drain(j, carry):
        back_copy(j).wait()
        for store in stores(j):
            store.wait()
        for kind in (0, 1):

            @pl.when(has_right)
            def _(kind=kind):
                along(me, kind, j, 1, True).wait_send()

            @pl.when(has_left)
            def _(kind=kind):
                along(me, kind, j, -1, True).wait_send()

        for distance in range(1, n):
            for step in (1, -1):
                origin = me - step * distance
                there = (origin >= 0) if step > 0 else (origin < n)
                on = has_right if step > 0 else has_left

                @pl.when(there & on)
                def _(origin=origin, step=step):
                    for kind in (0, 1):
                        along(origin, kind, j, step).wait_send()

        return carry

    lax.fori_loop(0, parts, drain, 0)

    for distance in range(n):
        for step in (1, -1):
            if distance == 0 or distance < n - 1:
                origin = me - step * distance
                there = (origin >= 0) if step > 0 else (origin < n)
                on = has_right if step > 0 else has_left

                @pl.when(there & on)
                def _(origin=origin, step=step):
                    factor_along(origin, step).wait_send()


def place_kernel(*refs):
    copies = []
    for i in range(3):
        source, target, sem = refs[i], refs[3 + i], refs[6]
        height = source.shape[0]
        pieces = 3 if height % 48 == 0 else 1
        for piece in range(pieces):
            span = pl.ds(piece * (height // pieces), height // pieces)
            copies.append(pltpu.make_async_copy(source.at[span], target.at[span], sem.at[i, piece]))
    for copy in copies:
        copy.start()
    for copy in copies:
        copy.wait()


def gathered(stash, back_in, down_proj, up_proj, gain, sent_to, sent_count, recv_from, back_live):
    sections, n = lax.axis_size("section"), lax.axis_size("peer")
    slots, micro, width = stash.shape[2:]
    rows = slots * micro
    rank = down_proj.shape[1]
    parts = 4
    packed = -(-(2 * rank + 3) // LANES) * LANES
    hbm = pl.BlockSpec(memory_space=pltpu.HBM)
    dma = pltpu.SemaphoreType.DMA
    results = pl.pallas_call(
        functools.partial(gather_kernel, sections, n, parts),
        out_shape=(
            jax.ShapeDtypeStruct((rows, width), jnp.bfloat16),
            jax.ShapeDtypeStruct((rank, width), jnp.bfloat16),
            jax.ShapeDtypeStruct((rank, width), jnp.bfloat16),
        ),
        in_specs=[hbm] * 9,
        out_specs=(hbm, hbm, hbm),
        scratch_shapes=[
            pltpu.VMEM((n, 2, rows, width), jnp.bfloat16),
            pltpu.VMEM((n, rows, packed), jnp.bfloat16),
            pltpu.VMEM((WIDE, width), jnp.bfloat16),
            pltpu.VMEM((WIDE, width), jnp.bfloat16),
            pltpu.VMEM((rows, LANES), jnp.float32),
            pltpu.VMEM((rows, LANES), jnp.float32),
            pltpu.VMEM((rows, width), jnp.bfloat16),
            pltpu.VMEM((rank, width), jnp.bfloat16),
            pltpu.VMEM((rank, width), jnp.bfloat16),
            pltpu.VMEM((1, width), jnp.float32),
            pltpu.SMEM(sent_to.shape, jnp.int32),
            pltpu.SMEM(sent_count.shape, jnp.int32),
            pltpu.SMEM(recv_from.shape, jnp.int32),
            pltpu.SMEM(back_live.shape, jnp.int32),
            dma((9,)),
            dma((n, 2, parts)),
            dma((n, 2, parts)),
            dma((n, 2, parts)),
            dma((n,)),
            dma((n,)),
            dma((n,)),
            dma((2,)),
            dma((parts,)),
            dma((parts,)),
            dma((2, parts)),
        ],
        compiler_params=pltpu.CompilerParams(
            collective_id=0, has_side_effects=True, vmem_limit_bytes=60 * 1024 * 1024
        ),
        cost_estimate=pl.CostEstimate(
            flops=10 * n * rows * rank * width, bytes_accessed=16 * rank * width, transcendentals=0
        ),
    )(
        stash.reshape(rows, width),
        back_in.reshape(rows, width),
        down_proj[0],
        up_proj[0],
        gain,
        sent_to,
        sent_count,
        recv_from,
        back_live,
    )
    returned, grad_down, grad_up = pl.pallas_call(
        place_kernel,
        out_shape=[jax.ShapeDtypeStruct(r.shape, r.dtype) for r in results],
        in_specs=[hbm] * 3,
        out_specs=[hbm] * 3,
        scratch_shapes=[dma((3, 3))],
        compiler_params=pltpu.CompilerParams(vmem_limit_bytes=60 * 1024 * 1024),
    )(*results)
    return returned.reshape(stash.shape), grad_down[None], grad_up[None]


def by_size(stash, *rest):
    n, sections = lax.axis_size("peer"), lax.axis_size("section")
    rows = stash.shape[2] * stash.shape[3]
    few = n * rows <= LANES and n > 2 and sections > 2
    return (gathered if few else on_device)(stash, *rest)


def solution(mesh):
    placed = (
        P("section", "peer", None, None, None),
        P("section", "peer", None, None, None),
        P("section", None, None),
        P("section", None, None),
        P("section", None),
        P("section", "peer", None),
        P("section", "peer"),
        P("section", "peer", None),
        P("section", "peer", None),
    )
    return jax.shard_map(
        by_size,
        mesh=mesh,
        in_specs=placed,
        out_specs=(
            P("section", "peer", None, None, None),
            P("section", None, None),
            P("section", None, None),
        ),
        check_vma=False,
    )
```

```python
import functools

import jax
import jax.numpy as jnp
from jax import lax
from jax.experimental import pallas as pl
from jax.experimental.pallas import tpu as pltpu
from jax.sharding import PartitionSpec as P

MESH = pl.DeviceIdType.MESH
LANES = 128
WIDE = 256

epsilon = 1e-05


def passed_along(block, axis, distance):
    devices = range(lax.axis_size(axis))
    route = [((i - distance) % len(devices), i) for i in devices]
    return lax.ppermute(block, axis, route)


def compact(blocks, targets, live_count):
    peer_count = blocks.shape[0]
    send_slots = targets.shape[0]
    peer_index = jnp.arange(peer_count, dtype=jnp.int32)
    slot_index = jnp.arange(send_slots, dtype=jnp.int32)
    selector = (
        (targets[:, None] == peer_index[None, :]) & (slot_index[:, None] < live_count)
    ).astype(jnp.bfloat16)
    flat = blocks.reshape(peer_count, -1)
    packed = jnp.dot(selector, flat, preferred_element_type=jnp.float32).astype(jnp.bfloat16)
    return packed.reshape((send_slots,) + blocks.shape[1:])


def on_device(stash, back_in, down_proj, up_proj, gain, sent_to, sent_count, recv_from, back_live):
    peer_count = lax.axis_size("peer")
    live_slots = back_live[0, 0]
    slot_mask = live_slots.astype(jnp.bfloat16)[:, None, None]
    slot_count = stash.shape[2]
    micro_rows = stash.shape[3]
    model_width = stash.shape[4]
    stored = (stash[0, 0] * slot_mask).reshape(slot_count * micro_rows, model_width)
    incoming = (back_in[0, 0] * slot_mask).reshape(slot_count * micro_rows, model_width)
    section_gain = gain[0]
    down_local = down_proj[0]
    up_local = up_proj[0]
    stored_f = stored.astype(jnp.float32)
    inverse = lax.rsqrt(jnp.mean(stored_f * stored_f, axis=-1, keepdims=True) + epsilon)
    unit_rows = stored_f * inverse
    normed = (unit_rows * section_gain).astype(jnp.bfloat16)
    contract_last = (((1,), (1,)), ((), ()))
    contract_rows = (((0,), (0,)), ((), ()))
    preact = lax.dot_general(normed, down_local, contract_last, preferred_element_type=jnp.float32)
    sigmoid_pre = jax.nn.sigmoid(preact)
    activation = (preact * sigmoid_pre).astype(jnp.bfloat16)
    back_act = lax.dot_general(
        incoming, up_local, contract_last, preferred_element_type=jnp.float32
    )
    back_pre = (back_act * (sigmoid_pre * (1.0 + preact * (1.0 - sigmoid_pre)))).astype(
        jnp.bfloat16
    )
    back_norm = jnp.dot(back_pre, down_local, preferred_element_type=jnp.float32) * section_gain
    input_grad = incoming.astype(jnp.float32) + inverse * (
        back_norm - unit_rows * jnp.mean(back_norm * unit_rows, axis=-1, keepdims=True)
    )
    input_grad = input_grad.astype(jnp.bfloat16)
    peer_index = jnp.arange(peer_count, dtype=jnp.int32)
    spreader = (
        (recv_from[0, 0][None, :] == peer_index[:, None]) & (live_slots[None, :] == 1)
    ).astype(jnp.bfloat16)
    by_sender = jnp.dot(
        spreader, input_grad.reshape(slot_count, -1), preferred_element_type=jnp.float32
    ).astype(jnp.bfloat16)
    by_sender = by_sender.reshape(peer_count, micro_rows, model_width)
    exchanged = lax.all_to_all(by_sender, "peer", split_axis=0, concat_axis=0, tiled=True)
    arrived = passed_along(exchanged, "section", -1)
    returned = compact(arrived, sent_to[0, 0], sent_count[0, 0])
    part_down = (
        lax.dot_general(back_pre, normed, contract_rows, preferred_element_type=jnp.float32)
        .astype(jnp.bfloat16)
        .astype(jnp.float32)
    )
    part_up = (
        lax.dot_general(activation, incoming, contract_rows, preferred_element_type=jnp.float32)
        .astype(jnp.bfloat16)
        .astype(jnp.float32)
    )
    summed_down, summed_up = (
        lax.psum(part_down.astype(jnp.bfloat16), "peer").astype(jnp.float32),
        lax.psum(part_up.astype(jnp.bfloat16), "peer").astype(jnp.float32),
    )
    grad_down = (summed_down / peer_count).astype(jnp.bfloat16)
    grad_up = (summed_up / peer_count).astype(jnp.bfloat16)
    return (returned[None, None], grad_down[None], grad_up[None])


def gather_kernel(
    sections,
    n,
    parts,
    stash,
    back_in,
    down,
    up,
    gain_in,
    sent_to_in,
    sent_count_in,
    recv_from_in,
    back_live_in,
    returned,
    grad_down_out,
    grad_up_out,
    rows_all,
    factors,
    w_down,
    w_up,
    asked,
    wanted,
    picked,
    grad_down,
    grad_up,
    gain_ref,
    sent_to,
    sent_count,
    recv_from,
    back_live,
    local_sem,
    right_sem,
    left_sem,
    recv_sem,
    fac_right,
    fac_left,
    fac_recv,
    want_sem,
    back_send,
    back_recv,
    out_sem,
):
    section = lax.axis_index("section")
    me = lax.axis_index("peer")
    before = lax.rem(section + sections - 1, sections)
    after = lax.rem(section + 1, sections)
    rows, width = stash.shape
    rank = down.shape[0]
    part = width // parts
    has_left, has_right = me > 0, me < n - 1

    def cols(j):
        return pl.ds(pl.multiple_of(j * part, part), part)

    def along(origin, kind, j, step, own=False):
        view = rows_all.at[origin, kind, :, cols(j)]
        source = (stash, back_in)[kind].at[:, cols(j)] if own else view
        return pltpu.make_async_remote_copy(
            src_ref=source,
            dst_ref=view,
            send_sem=(right_sem if step > 0 else left_sem).at[origin, kind, j],
            recv_sem=recv_sem.at[origin, kind, j],
            device_id=(section, me + step),
            device_id_type=MESH,
        )

    def factor_along(origin, step):
        return pltpu.make_async_remote_copy(
            src_ref=factors.at[origin],
            dst_ref=factors.at[origin],
            send_sem=(fac_right if step > 0 else fac_left).at[origin],
            recv_sem=fac_recv.at[origin],
            device_id=(section, me + step),
            device_id_type=MESH,
        )

    def want_copy():
        return pltpu.make_async_remote_copy(
            src_ref=asked,
            dst_ref=wanted,
            send_sem=want_sem.at[0],
            recv_sem=want_sem.at[1],
            device_id=(after, me),
            device_id_type=MESH,
        )

    def back_copy(j):
        return pltpu.make_async_remote_copy(
            src_ref=picked.at[:, cols(j)],
            dst_ref=returned.at[:, cols(j)],
            send_sem=back_send.at[j],
            recv_sem=back_recv.at[j],
            device_id=(before, me),
            device_id_type=MESH,
        )

    small = [
        pltpu.make_async_copy(sent_to_in, sent_to, local_sem.at[5]),
        pltpu.make_async_copy(sent_count_in, sent_count, local_sem.at[6]),
        pltpu.make_async_copy(recv_from_in, recv_from, local_sem.at[7]),
        pltpu.make_async_copy(back_live_in, back_live, local_sem.at[8]),
    ]
    def stores(j):
        return (
            pltpu.make_async_copy(
                grad_down.at[:, cols(j)], grad_down_out.at[:, cols(j)], out_sem.at[0, j]
            ),
            pltpu.make_async_copy(
                grad_up.at[:, cols(j)], grad_up_out.at[:, cols(j)], out_sem.at[1, j]
            ),
        )

    loads = [
        pltpu.make_async_copy(stash, rows_all.at[me, 0], local_sem.at[0]),
        pltpu.make_async_copy(back_in, rows_all.at[me, 1], local_sem.at[1]),
        pltpu.make_async_copy(down, w_down.at[pl.ds(0, rank)], local_sem.at[2]),
        pltpu.make_async_copy(up, w_up.at[pl.ds(0, rank)], local_sem.at[3]),
        pltpu.make_async_copy(gain_in, gain_ref, local_sem.at[4]),
    ]
    for load in small + loads:
        load.start()

    barrier = pltpu.get_barrier_semaphore()
    for other in (before, after):
        pl.semaphore_signal(barrier, inc=1, device_id=(other, me), device_id_type=MESH)

    @pl.when(has_left)
    def _():
        pl.semaphore_signal(barrier, inc=1, device_id=(section, me - 1), device_id_type=MESH)

    @pl.when(has_right)
    def _():
        pl.semaphore_signal(barrier, inc=1, device_id=(section, me + 1), device_id_type=MESH)

    @pl.when(has_left & has_right)
    def _():
        pl.semaphore_wait(barrier, 4)

    @pl.when(jnp.logical_not(has_left & has_right))
    def _():
        pl.semaphore_wait(barrier, 3)

    for j in range(parts):
        for kind in (0, 1):

            @pl.when(has_right)
            def _(j=j, kind=kind):
                along(me, kind, j, 1, True).start()

            @pl.when(has_left)
            def _(j=j, kind=kind):
                along(me, kind, j, -1, True).start()

    for load in small:
        load.wait()
    slots = sent_to.shape[2]
    micro = rows // slots
    at_row = lax.broadcasted_iota(jnp.int32, (rows, LANES), 0)
    at_lane = lax.broadcasted_iota(jnp.int32, (rows, LANES), 1)
    lane_peer = jnp.zeros((rows, LANES), jnp.int32)
    for a in range(1, n):
        lane_peer += jnp.where(at_lane >= a * rows, 1, 0)
    target = jnp.full((rows, LANES), -1, jnp.int32)
    for k in range(slots):
        here = (at_row >= k * micro) & (at_row < (k + 1) * micro)
        target = jnp.where(here & (sent_count[0, 0] > k), sent_to[0, 0, k], target)
    same = lax.rem(at_lane, micro) == lax.rem(at_row, micro)
    asked[...] = jnp.where(same & (lane_peer == target), 1.0, 0.0)
    want_copy().start()

    w_down[pl.ds(rank, WIDE - rank), :] = jnp.zeros((WIDE - rank, width), jnp.bfloat16)
    w_up[pl.ds(rank, WIDE - rank), :] = jnp.zeros((WIDE - rank, width), jnp.bfloat16)
    for load in loads:
        load.wait()

    def square_part(j, total):
        block = rows_all[me, 0, :, cols(j)].astype(jnp.float32)
        return total + jnp.sum(block * block, axis=-1, keepdims=True)

    squares = lax.fori_loop(0, parts, square_part, jnp.zeros((rows, 1), jnp.float32))
    inverse = lax.rsqrt(squares / width + epsilon)
    contract_last = (((1,), (1,)), ((), ()))

    def project_part(j, carry):
        pre, back = carry
        block = rows_all[me, 0, :, cols(j)].astype(jnp.float32)
        normed = (block * inverse * gain_ref[:, cols(j)]).astype(jnp.bfloat16)
        pre = pre + lax.dot_general(
            normed, w_down[:, cols(j)], contract_last, preferred_element_type=jnp.float32
        )
        back = back + lax.dot_general(
            rows_all[me, 1, :, cols(j)],
            w_up[:, cols(j)],
            contract_last,
            preferred_element_type=jnp.float32,
        )
        return pre, back

    empty = jnp.zeros((rows, WIDE), jnp.float32)
    preact, back_act = lax.fori_loop(0, parts, project_part, (empty, empty))
    row_only = lax.broadcasted_iota(jnp.int32, (rows, 1), 0)
    live = jnp.zeros((rows, 1), jnp.float32)
    code = jnp.zeros((rows, 1), jnp.float32)
    for k in range(slots):
        held = back_live[0, 0, k]
        here = (row_only >= k * micro) & (row_only < (k + 1) * micro)
        live = jnp.where(here, held.astype(jnp.float32), live)
        code = jnp.where(here, ((recv_from[0, 0, k] + 1) * held).astype(jnp.float32), code)
    sigmoid_pre = jax.nn.sigmoid(preact)
    activation = preact * sigmoid_pre * live
    back_pre = back_act * (sigmoid_pre * (1.0 + preact * (1.0 - sigmoid_pre))) * live
    slope = jnp.sum(back_pre * preact, axis=-1, keepdims=True) * (inverse * inverse / width)
    slope_high = slope.astype(jnp.bfloat16).astype(jnp.float32)
    packed = factors.shape[2]
    extra = jnp.zeros((rows, packed - WIDE), jnp.float32)
    lane = lax.broadcasted_iota(jnp.int32, (rows, packed), 1)
    body = jnp.concatenate([back_pre * inverse, extra], axis=1)
    body += pltpu.roll(jnp.concatenate([activation, extra], axis=1), rank, 1)
    for at, value in enumerate((slope_high, slope - slope_high, code)):
        body = jnp.where(lane == 2 * rank + at, value, body)
    factors[me] = body.astype(jnp.bfloat16)

    @pl.when(has_right)
    def _():
        factor_along(me, 1).start()

    @pl.when(has_left)
    def _():
        factor_along(me, -1).start()

    def arrivals(distance, j):
        for step in (1, -1):
            origin = me - step * distance
            there = (origin >= 0) if step > 0 else (origin < n)
            on = has_right if step > 0 else has_left

            @pl.when(there)
            def _(origin=origin, step=step, on=on):
                for kind in (0, 1):
                    along(origin, kind, j, step).wait_recv()

                    @pl.when(on)
                    def _(kind=kind):
                        along(origin, kind, j, step).start()

    def factor_arrivals(distance):
        for step in (1, -1):
            origin = me - step * distance
            there = (origin >= 0) if step > 0 else (origin < n)
            on = has_right if step > 0 else has_left

            @pl.when(there)
            def _(origin=origin, step=step, on=on):
                factor_along(origin, step).wait_recv()

                @pl.when(on)
                def _():
                    factor_along(origin, step).start()

    for distance in range(1, n):
        arrivals(distance, 0)
        factor_arrivals(distance)
        if distance < n - 1:
            for j in range(1, parts):
                arrivals(distance, j)

    want_copy().wait()
    body_all = jnp.concatenate([factors[a].astype(jnp.float32) for a in range(n)], axis=0)
    body_t = jnp.transpose(body_all)
    mine = (me + 1).astype(jnp.float32)
    codes_all = body_t[2 * rank + 2 : 2 * rank + 3]
    select = jnp.where(codes_all == mine, wanted[...][:, : n * rows], 0.0)
    chosen = jnp.dot(
        select.astype(jnp.bfloat16), body_all.astype(jnp.bfloat16), preferred_element_type=jnp.float32
    )
    chosen_back = chosen[:, :WIDE].astype(jnp.bfloat16)
    slope_lane = (lane == 2 * rank) | (lane == 2 * rank + 1)
    chosen_slope = jnp.sum(jnp.where(slope_lane, chosen, 0.0), axis=-1, keepdims=True)
    down_pick = jnp.concatenate([select, body_t[:rank]], axis=0).astype(jnp.bfloat16)
    up_pick = jnp.concatenate([select, body_t[rank : 2 * rank]], axis=0).astype(jnp.bfloat16)

    def finish(j, carry):
        @pl.when(j > 0)
        def _():
            arrivals(n - 1, j)

        gain = gain_ref[:, cols(j)]

        def whole(kind):
            blocks = [rows_all[a, kind, :, cols(j)].astype(jnp.float32) for a in range(n)]
            return jnp.concatenate(blocks, axis=0).astype(jnp.bfloat16)

        stash_all, back_all = whole(0), whole(1)
        through = jnp.dot(chosen_back, w_down[:, cols(j)], preferred_element_type=jnp.float32)
        from_stash = jnp.dot(down_pick, stash_all, preferred_element_type=jnp.float32)
        from_back = jnp.dot(up_pick, back_all, preferred_element_type=jnp.float32)
        out = from_back[:rows] + through * gain - chosen_slope * from_stash[:rows]
        picked[:, cols(j)] = out.astype(jnp.bfloat16)
        back_copy(j).start()
        grad_down[:, cols(j)] = (from_stash[rows:] * (gain / n)).astype(jnp.bfloat16)
        grad_up[:, cols(j)] = (from_back[rows:] / n).astype(jnp.bfloat16)
        for store in stores(j):
            store.start()
        return carry

    lax.fori_loop(0, parts, finish, 0)

    def drain(j, carry):
        back_copy(j).wait()
        for store in stores(j):
            store.wait()
        for kind in (0, 1):

            @pl.when(has_right)
            def _(kind=kind):
                along(me, kind, j, 1, True).wait_send()

            @pl.when(has_left)
            def _(kind=kind):
                along(me, kind, j, -1, True).wait_send()

        for distance in range(1, n):
            for step in (1, -1):
                origin = me - step * distance
                there = (origin >= 0) if step > 0 else (origin < n)
                on = has_right if step > 0 else has_left

                @pl.when(there & on)
                def _(origin=origin, step=step):
                    for kind in (0, 1):
                        along(origin, kind, j, step).wait_send()

        return carry

    lax.fori_loop(0, parts, drain, 0)

    for distance in range(n):
        for step in (1, -1):
            if distance == 0 or distance < n - 1:
                origin = me - step * distance
                there = (origin >= 0) if step > 0 else (origin < n)
                on = has_right if step > 0 else has_left

                @pl.when(there & on)
                def _(origin=origin, step=step):
                    factor_along(origin, step).wait_send()


def place_kernel(*refs):
    sources, targets, held, (read_sem, write_sem) = refs[:3], refs[3:6], refs[6:9], refs[9:]
    reads, writes = [], []
    for i in (1, 2, 0):
        height = sources[i].shape[0]
        pieces = 3 if height % 48 == 0 else 1
        for piece in range(pieces):
            span = pl.ds(piece * (height // pieces), height // pieces)
            inside = held[i].at[span]
            reads.append(
                pltpu.make_async_copy(sources[i].at[span], inside, read_sem.at[i, piece])
            )
            writes.append(
                pltpu.make_async_copy(inside, targets[i].at[span], write_sem.at[i, piece])
            )
    for read in reads:
        read.start()
    for read, write in zip(reads, writes):
        read.wait()
        write.start()
    for write in writes:
        write.wait()


def gathered(stash, back_in, down_proj, up_proj, gain, sent_to, sent_count, recv_from, back_live):
    sections, n = lax.axis_size("section"), lax.axis_size("peer")
    slots, micro, width = stash.shape[2:]
    rows = slots * micro
    rank = down_proj.shape[1]
    parts = 4
    packed = -(-(2 * rank + 3) // LANES) * LANES
    hbm = pl.BlockSpec(memory_space=pltpu.HBM)
    dma = pltpu.SemaphoreType.DMA
    results = pl.pallas_call(
        functools.partial(gather_kernel, sections, n, parts),
        out_shape=(
            jax.ShapeDtypeStruct((rows, width), jnp.bfloat16),
            jax.ShapeDtypeStruct((rank, width), jnp.bfloat16),
            jax.ShapeDtypeStruct((rank, width), jnp.bfloat16),
        ),
        in_specs=[hbm] * 9,
        out_specs=(hbm, hbm, hbm),
        scratch_shapes=[
            pltpu.VMEM((n, 2, rows, width), jnp.bfloat16),
            pltpu.VMEM((n, rows, packed), jnp.bfloat16),
            pltpu.VMEM((WIDE, width), jnp.bfloat16),
            pltpu.VMEM((WIDE, width), jnp.bfloat16),
            pltpu.VMEM((rows, LANES), jnp.float32),
            pltpu.VMEM((rows, LANES), jnp.float32),
            pltpu.VMEM((rows, width), jnp.bfloat16),
            pltpu.VMEM((rank, width), jnp.bfloat16),
            pltpu.VMEM((rank, width), jnp.bfloat16),
            pltpu.VMEM((1, width), jnp.float32),
            pltpu.SMEM(sent_to.shape, jnp.int32),
            pltpu.SMEM(sent_count.shape, jnp.int32),
            pltpu.SMEM(recv_from.shape, jnp.int32),
            pltpu.SMEM(back_live.shape, jnp.int32),
            dma((9,)),
            dma((n, 2, parts)),
            dma((n, 2, parts)),
            dma((n, 2, parts)),
            dma((n,)),
            dma((n,)),
            dma((n,)),
            dma((2,)),
            dma((parts,)),
            dma((parts,)),
            dma((2, parts)),
        ],
        compiler_params=pltpu.CompilerParams(
            collective_id=0, has_side_effects=True, vmem_limit_bytes=60 * 1024 * 1024
        ),
        cost_estimate=pl.CostEstimate(
            flops=10 * n * rows * rank * width, bytes_accessed=16 * rank * width, transcendentals=0
        ),
    )(
        stash.reshape(rows, width),
        back_in.reshape(rows, width),
        down_proj[0],
        up_proj[0],
        gain,
        sent_to,
        sent_count,
        recv_from,
        back_live,
    )
    returned, grad_down, grad_up = pl.pallas_call(
        place_kernel,
        out_shape=[jax.ShapeDtypeStruct(r.shape, r.dtype) for r in results],
        in_specs=[hbm] * 3,
        out_specs=[hbm] * 3,
        scratch_shapes=[pltpu.VMEM(r.shape, r.dtype) for r in results] + [dma((3, 3))] * 2,
        compiler_params=pltpu.CompilerParams(vmem_limit_bytes=60 * 1024 * 1024),
    )(*results)
    return returned.reshape(stash.shape), grad_down[None], grad_up[None]


def by_size(stash, *rest):
    n, sections = lax.axis_size("peer"), lax.axis_size("section")
    rows = stash.shape[2] * stash.shape[3]
    few = n * rows <= LANES and n > 2 and sections > 2
    return (gathered if few else on_device)(stash, *rest)


def solution(mesh):
    placed = (
        P("section", "peer", None, None, None),
        P("section", "peer", None, None, None),
        P("section", None, None),
        P("section", None, None),
        P("section", None),
        P("section", "peer", None),
        P("section", "peer"),
        P("section", "peer", None),
        P("section", "peer", None),
    )
    return jax.shard_map(
        by_size,
        mesh=mesh,
        in_specs=placed,
        out_specs=(
            P("section", "peer", None, None, None),
            P("section", None, None),
            P("section", None, None),
        ),
        check_vma=False,
    )
```

```python
import functools

import jax
import jax.numpy as jnp
from jax import lax
from jax.experimental import pallas as pl
from jax.experimental.pallas import tpu as pltpu
from jax.sharding import PartitionSpec as P

MESH = pl.DeviceIdType.MESH
LANES = 128
WIDE = 256

epsilon = 1e-05


def passed_along(block, axis, distance):
    devices = range(lax.axis_size(axis))
    route = [((i - distance) % len(devices), i) for i in devices]
    return lax.ppermute(block, axis, route)


def compact(blocks, targets, live_count):
    peer_count = blocks.shape[0]
    send_slots = targets.shape[0]
    peer_index = jnp.arange(peer_count, dtype=jnp.int32)
    slot_index = jnp.arange(send_slots, dtype=jnp.int32)
    selector = (
        (targets[:, None] == peer_index[None, :]) & (slot_index[:, None] < live_count)
    ).astype(jnp.bfloat16)
    flat = blocks.reshape(peer_count, -1)
    packed = jnp.dot(selector, flat, preferred_element_type=jnp.float32).astype(jnp.bfloat16)
    return packed.reshape((send_slots,) + blocks.shape[1:])


def on_device(stash, back_in, down_proj, up_proj, gain, sent_to, sent_count, recv_from, back_live):
    peer_count = lax.axis_size("peer")
    live_slots = back_live[0, 0]
    slot_mask = live_slots.astype(jnp.bfloat16)[:, None, None]
    slot_count = stash.shape[2]
    micro_rows = stash.shape[3]
    model_width = stash.shape[4]
    stored = (stash[0, 0] * slot_mask).reshape(slot_count * micro_rows, model_width)
    incoming = (back_in[0, 0] * slot_mask).reshape(slot_count * micro_rows, model_width)
    section_gain = gain[0]
    down_local = down_proj[0]
    up_local = up_proj[0]
    stored_f = stored.astype(jnp.float32)
    inverse = lax.rsqrt(jnp.mean(stored_f * stored_f, axis=-1, keepdims=True) + epsilon)
    unit_rows = stored_f * inverse
    normed = (unit_rows * section_gain).astype(jnp.bfloat16)
    contract_last = (((1,), (1,)), ((), ()))
    contract_rows = (((0,), (0,)), ((), ()))
    preact = lax.dot_general(normed, down_local, contract_last, preferred_element_type=jnp.float32)
    sigmoid_pre = jax.nn.sigmoid(preact)
    activation = (preact * sigmoid_pre).astype(jnp.bfloat16)
    back_act = lax.dot_general(
        incoming, up_local, contract_last, preferred_element_type=jnp.float32
    )
    back_pre = (back_act * (sigmoid_pre * (1.0 + preact * (1.0 - sigmoid_pre)))).astype(
        jnp.bfloat16
    )
    back_norm = jnp.dot(back_pre, down_local, preferred_element_type=jnp.float32) * section_gain
    input_grad = incoming.astype(jnp.float32) + inverse * (
        back_norm - unit_rows * jnp.mean(back_norm * unit_rows, axis=-1, keepdims=True)
    )
    input_grad = input_grad.astype(jnp.bfloat16)
    peer_index = jnp.arange(peer_count, dtype=jnp.int32)
    spreader = (
        (recv_from[0, 0][None, :] == peer_index[:, None]) & (live_slots[None, :] == 1)
    ).astype(jnp.bfloat16)
    by_sender = jnp.dot(
        spreader, input_grad.reshape(slot_count, -1), preferred_element_type=jnp.float32
    ).astype(jnp.bfloat16)
    by_sender = by_sender.reshape(peer_count, micro_rows, model_width)
    exchanged = lax.all_to_all(by_sender, "peer", split_axis=0, concat_axis=0, tiled=True)
    arrived = passed_along(exchanged, "section", -1)
    returned = compact(arrived, sent_to[0, 0], sent_count[0, 0])
    part_down = (
        lax.dot_general(back_pre, normed, contract_rows, preferred_element_type=jnp.float32)
        .astype(jnp.bfloat16)
        .astype(jnp.float32)
    )
    part_up = (
        lax.dot_general(activation, incoming, contract_rows, preferred_element_type=jnp.float32)
        .astype(jnp.bfloat16)
        .astype(jnp.float32)
    )
    summed_down, summed_up = (
        lax.psum(part_down.astype(jnp.bfloat16), "peer").astype(jnp.float32),
        lax.psum(part_up.astype(jnp.bfloat16), "peer").astype(jnp.float32),
    )
    grad_down = (summed_down / peer_count).astype(jnp.bfloat16)
    grad_up = (summed_up / peer_count).astype(jnp.bfloat16)
    return (returned[None, None], grad_down[None], grad_up[None])


def gather_kernel(
    sections,
    n,
    parts,
    stash,
    back_in,
    down,
    up,
    gain_in,
    sent_to_in,
    sent_count_in,
    recv_from_in,
    back_live_in,
    returned,
    grad_down_out,
    grad_up_out,
    rows_all,
    factors,
    w_down,
    w_up,
    asked,
    wanted,
    picked,
    grad_down,
    grad_up,
    gain_ref,
    sent_to,
    sent_count,
    recv_from,
    back_live,
    local_sem,
    right_sem,
    left_sem,
    recv_sem,
    fac_right,
    fac_left,
    fac_recv,
    want_sem,
    back_send,
    back_recv,
    out_sem,
):
    section = lax.axis_index("section")
    me = lax.axis_index("peer")
    before = lax.rem(section + sections - 1, sections)
    after = lax.rem(section + 1, sections)
    rows, width = stash.shape
    rank = down.shape[0]
    part = width // parts
    has_left, has_right = me > 0, me < n - 1

    def cols(j):
        return pl.ds(pl.multiple_of(j * part, part), part)

    def along(origin, kind, j, step, own=False):
        view = rows_all.at[origin, kind, :, cols(j)]
        source = (stash, back_in)[kind].at[:, cols(j)] if own else view
        return pltpu.make_async_remote_copy(
            src_ref=source,
            dst_ref=view,
            send_sem=(right_sem if step > 0 else left_sem).at[origin, kind, j],
            recv_sem=recv_sem.at[origin, kind, j],
            device_id=(section, me + step),
            device_id_type=MESH,
        )

    def factor_along(origin, step):
        return pltpu.make_async_remote_copy(
            src_ref=factors.at[origin],
            dst_ref=factors.at[origin],
            send_sem=(fac_right if step > 0 else fac_left).at[origin],
            recv_sem=fac_recv.at[origin],
            device_id=(section, me + step),
            device_id_type=MESH,
        )

    def want_copy():
        return pltpu.make_async_remote_copy(
            src_ref=asked,
            dst_ref=wanted,
            send_sem=want_sem.at[0],
            recv_sem=want_sem.at[1],
            device_id=(after, me),
            device_id_type=MESH,
        )

    def back_copy(j):
        return pltpu.make_async_remote_copy(
            src_ref=picked.at[:, cols(j)],
            dst_ref=returned.at[:, cols(j)],
            send_sem=back_send.at[j],
            recv_sem=back_recv.at[j],
            device_id=(before, me),
            device_id_type=MESH,
        )

    small = [
        pltpu.make_async_copy(sent_to_in, sent_to, local_sem.at[5]),
        pltpu.make_async_copy(sent_count_in, sent_count, local_sem.at[6]),
        pltpu.make_async_copy(recv_from_in, recv_from, local_sem.at[7]),
        pltpu.make_async_copy(back_live_in, back_live, local_sem.at[8]),
    ]
    def stores(j):
        return (
            pltpu.make_async_copy(
                grad_down.at[:, cols(j)], grad_down_out.at[:, cols(j)], out_sem.at[0, j]
            ),
            pltpu.make_async_copy(
                grad_up.at[:, cols(j)], grad_up_out.at[:, cols(j)], out_sem.at[1, j]
            ),
        )

    loads = [
        pltpu.make_async_copy(stash, rows_all.at[me, 0], local_sem.at[0]),
        pltpu.make_async_copy(back_in, rows_all.at[me, 1], local_sem.at[1]),
        pltpu.make_async_copy(down, w_down.at[pl.ds(0, rank)], local_sem.at[2]),
        pltpu.make_async_copy(up, w_up.at[pl.ds(0, rank)], local_sem.at[3]),
        pltpu.make_async_copy(gain_in, gain_ref, local_sem.at[4]),
    ]
    for load in small + loads:
        load.start()

    barrier = pltpu.get_barrier_semaphore()
    for other in (before, after):
        pl.semaphore_signal(barrier, inc=1, device_id=(other, me), device_id_type=MESH)

    @pl.when(has_left)
    def _():
        pl.semaphore_signal(barrier, inc=1, device_id=(section, me - 1), device_id_type=MESH)

    @pl.when(has_right)
    def _():
        pl.semaphore_signal(barrier, inc=1, device_id=(section, me + 1), device_id_type=MESH)

    @pl.when(has_left & has_right)
    def _():
        pl.semaphore_wait(barrier, 4)

    @pl.when(jnp.logical_not(has_left & has_right))
    def _():
        pl.semaphore_wait(barrier, 3)

    def send_own(j, carry):
        for kind in (0, 1):

            @pl.when(has_right)
            def _(kind=kind):
                along(me, kind, j, 1, True).start()

            @pl.when(has_left)
            def _(kind=kind):
                along(me, kind, j, -1, True).start()

        return carry

    lax.fori_loop(0, parts, send_own, 0)

    for load in small:
        load.wait()
    slots = sent_to.shape[2]
    micro = rows // slots
    at_row = lax.broadcasted_iota(jnp.int32, (rows, LANES), 0)
    at_lane = lax.broadcasted_iota(jnp.int32, (rows, LANES), 1)
    lane_peer = jnp.zeros((rows, LANES), jnp.int32)
    for a in range(1, n):
        lane_peer += jnp.where(at_lane >= a * rows, 1, 0)
    target = jnp.full((rows, LANES), -1, jnp.int32)
    for k in range(slots):
        here = (at_row >= k * micro) & (at_row < (k + 1) * micro)
        target = jnp.where(here & (sent_count[0, 0] > k), sent_to[0, 0, k], target)
    same = lax.rem(at_lane, micro) == lax.rem(at_row, micro)
    asked[...] = jnp.where(same & (lane_peer == target), 1.0, 0.0)
    want_copy().start()

    w_down[pl.ds(rank, WIDE - rank), :] = jnp.zeros((WIDE - rank, width), jnp.bfloat16)
    w_up[pl.ds(rank, WIDE - rank), :] = jnp.zeros((WIDE - rank, width), jnp.bfloat16)
    for load in loads:
        load.wait()

    def square_part(j, total):
        block = rows_all[me, 0, :, cols(j)].astype(jnp.float32)
        return total + jnp.sum(block * block, axis=-1, keepdims=True)

    squares = lax.fori_loop(0, parts, square_part, jnp.zeros((rows, 1), jnp.float32))
    inverse = lax.rsqrt(squares / width + epsilon)
    contract_last = (((1,), (1,)), ((), ()))

    def project_part(j, carry):
        pre, back = carry
        block = rows_all[me, 0, :, cols(j)].astype(jnp.float32)
        normed = (block * inverse * gain_ref[:, cols(j)]).astype(jnp.bfloat16)
        pre = pre + lax.dot_general(
            normed, w_down[:, cols(j)], contract_last, preferred_element_type=jnp.float32
        )
        back = back + lax.dot_general(
            rows_all[me, 1, :, cols(j)],
            w_up[:, cols(j)],
            contract_last,
            preferred_element_type=jnp.float32,
        )
        return pre, back

    empty = jnp.zeros((rows, WIDE), jnp.float32)
    preact, back_act = lax.fori_loop(0, parts, project_part, (empty, empty))
    row_only = lax.broadcasted_iota(jnp.int32, (rows, 1), 0)
    live = jnp.zeros((rows, 1), jnp.float32)
    code = jnp.zeros((rows, 1), jnp.float32)
    for k in range(slots):
        held = back_live[0, 0, k]
        here = (row_only >= k * micro) & (row_only < (k + 1) * micro)
        live = jnp.where(here, held.astype(jnp.float32), live)
        code = jnp.where(here, ((recv_from[0, 0, k] + 1) * held).astype(jnp.float32), code)
    sigmoid_pre = jax.nn.sigmoid(preact)
    activation = preact * sigmoid_pre * live
    back_pre = back_act * (sigmoid_pre * (1.0 + preact * (1.0 - sigmoid_pre))) * live
    slope = jnp.sum(back_pre * preact, axis=-1, keepdims=True) * (inverse * inverse / width)
    slope_high = slope.astype(jnp.bfloat16).astype(jnp.float32)
    packed = factors.shape[2]
    extra = jnp.zeros((rows, packed - WIDE), jnp.float32)
    lane = lax.broadcasted_iota(jnp.int32, (rows, packed), 1)
    body = jnp.concatenate([back_pre * inverse, extra], axis=1)
    body += pltpu.roll(jnp.concatenate([activation, extra], axis=1), rank, 1)
    for at, value in enumerate((slope_high, slope - slope_high, code)):
        body = jnp.where(lane == 2 * rank + at, value, body)
    factors[me] = body.astype(jnp.bfloat16)

    @pl.when(has_right)
    def _():
        factor_along(me, 1).start()

    @pl.when(has_left)
    def _():
        factor_along(me, -1).start()

    def arrivals(distance, j):
        for step in (1, -1):
            origin = me - step * distance
            there = (origin >= 0) if step > 0 else (origin < n)
            on = has_right if step > 0 else has_left

            @pl.when(there)
            def _(origin=origin, step=step, on=on):
                for kind in (0, 1):
                    along(origin, kind, j, step).wait_recv()

                    @pl.when(on)
                    def _(kind=kind):
                        along(origin, kind, j, step).start()

    def factor_arrivals(distance):
        for step in (1, -1):
            origin = me - step * distance
            there = (origin >= 0) if step > 0 else (origin < n)
            on = has_right if step > 0 else has_left

            @pl.when(there)
            def _(origin=origin, step=step, on=on):
                factor_along(origin, step).wait_recv()

                @pl.when(on)
                def _():
                    factor_along(origin, step).start()

    def pass_on(distance, j, carry):
        arrivals(distance, j)
        return carry

    for distance in range(1, n):
        arrivals(distance, 0)
        factor_arrivals(distance)
        if distance < n - 1:
            lax.fori_loop(1, parts, functools.partial(pass_on, distance), 0)

    want_copy().wait()
    body_all = jnp.concatenate([factors[a].astype(jnp.float32) for a in range(n)], axis=0)
    body_t = jnp.transpose(body_all)
    mine = (me + 1).astype(jnp.float32)
    codes_all = body_t[2 * rank + 2 : 2 * rank + 3]
    select = jnp.where(codes_all == mine, wanted[...][:, : n * rows], 0.0)
    chosen = jnp.dot(
        select.astype(jnp.bfloat16), body_all.astype(jnp.bfloat16), preferred_element_type=jnp.float32
    )
    chosen_back = chosen[:, :WIDE].astype(jnp.bfloat16)
    slope_lane = (lane == 2 * rank) | (lane == 2 * rank + 1)
    chosen_slope = jnp.sum(jnp.where(slope_lane, chosen, 0.0), axis=-1, keepdims=True)
    down_pick = jnp.concatenate([select, body_t[:rank]], axis=0).astype(jnp.bfloat16)
    up_pick = jnp.concatenate([select, body_t[rank : 2 * rank]], axis=0).astype(jnp.bfloat16)

    def finish(j, carry):
        @pl.when(j > 0)
        def _():
            arrivals(n - 1, j)

        gain = gain_ref[:, cols(j)]

        def whole(kind):
            blocks = [rows_all[a, kind, :, cols(j)].astype(jnp.float32) for a in range(n)]
            return jnp.concatenate(blocks, axis=0).astype(jnp.bfloat16)

        stash_all, back_all = whole(0), whole(1)
        through = jnp.dot(chosen_back, w_down[:, cols(j)], preferred_element_type=jnp.float32)
        from_stash = jnp.dot(down_pick, stash_all, preferred_element_type=jnp.float32)
        from_back = jnp.dot(up_pick, back_all, preferred_element_type=jnp.float32)
        out = from_back[:rows] + through * gain - chosen_slope * from_stash[:rows]
        picked[:, cols(j)] = out.astype(jnp.bfloat16)
        back_copy(j).start()
        grad_down[:, cols(j)] = (from_stash[rows:] * (gain / n)).astype(jnp.bfloat16)
        grad_up[:, cols(j)] = (from_back[rows:] / n).astype(jnp.bfloat16)
        for store in stores(j):
            store.start()
        return carry

    lax.fori_loop(0, parts, finish, 0)

    def drain(j, carry):
        back_copy(j).wait()
        for store in stores(j):
            store.wait()
        for kind in (0, 1):

            @pl.when(has_right)
            def _(kind=kind):
                along(me, kind, j, 1, True).wait_send()

            @pl.when(has_left)
            def _(kind=kind):
                along(me, kind, j, -1, True).wait_send()

        for distance in range(1, n):
            for step in (1, -1):
                origin = me - step * distance
                there = (origin >= 0) if step > 0 else (origin < n)
                on = has_right if step > 0 else has_left

                @pl.when(there & on)
                def _(origin=origin, step=step):
                    for kind in (0, 1):
                        along(origin, kind, j, step).wait_send()

        return carry

    lax.fori_loop(0, parts, drain, 0)

    for distance in range(n):
        for step in (1, -1):
            if distance == 0 or distance < n - 1:
                origin = me - step * distance
                there = (origin >= 0) if step > 0 else (origin < n)
                on = has_right if step > 0 else has_left

                @pl.when(there & on)
                def _(origin=origin, step=step):
                    factor_along(origin, step).wait_send()


def place_kernel(*refs):
    sources, targets, held, (read_sem, write_sem) = refs[:3], refs[3:6], refs[6:9], refs[9:]
    reads, writes = [], []
    for i in (1, 2, 0):
        height = sources[i].shape[0]
        pieces = 3 if height % 48 == 0 else 1
        for piece in range(pieces):
            span = pl.ds(piece * (height // pieces), height // pieces)
            inside = held[i].at[span]
            reads.append(
                pltpu.make_async_copy(sources[i].at[span], inside, read_sem.at[i, piece])
            )
            writes.append(
                pltpu.make_async_copy(inside, targets[i].at[span], write_sem.at[i, piece])
            )
    for read in reads:
        read.start()
    for read, write in zip(reads, writes):
        read.wait()
        write.start()
    for write in writes:
        write.wait()


def gathered(stash, back_in, down_proj, up_proj, gain, sent_to, sent_count, recv_from, back_live):
    sections, n = lax.axis_size("section"), lax.axis_size("peer")
    slots, micro, width = stash.shape[2:]
    rows = slots * micro
    rank = down_proj.shape[1]
    parts = 10
    packed = -(-(2 * rank + 3) // LANES) * LANES
    hbm = pl.BlockSpec(memory_space=pltpu.HBM)
    dma = pltpu.SemaphoreType.DMA
    results = pl.pallas_call(
        functools.partial(gather_kernel, sections, n, parts),
        out_shape=(
            jax.ShapeDtypeStruct((rows, width), jnp.bfloat16),
            jax.ShapeDtypeStruct((rank, width), jnp.bfloat16),
            jax.ShapeDtypeStruct((rank, width), jnp.bfloat16),
        ),
        in_specs=[hbm] * 9,
        out_specs=(hbm, hbm, hbm),
        scratch_shapes=[
            pltpu.VMEM((n, 2, rows, width), jnp.bfloat16),
            pltpu.VMEM((n, rows, packed), jnp.bfloat16),
            pltpu.VMEM((WIDE, width), jnp.bfloat16),
            pltpu.VMEM((WIDE, width), jnp.bfloat16),
            pltpu.VMEM((rows, LANES), jnp.float32),
            pltpu.VMEM((rows, LANES), jnp.float32),
            pltpu.VMEM((rows, width), jnp.bfloat16),
            pltpu.VMEM((rank, width), jnp.bfloat16),
            pltpu.VMEM((rank, width), jnp.bfloat16),
            pltpu.VMEM((1, width), jnp.float32),
            pltpu.SMEM(sent_to.shape, jnp.int32),
            pltpu.SMEM(sent_count.shape, jnp.int32),
            pltpu.SMEM(recv_from.shape, jnp.int32),
            pltpu.SMEM(back_live.shape, jnp.int32),
            dma((9,)),
            dma((n, 2, parts)),
            dma((n, 2, parts)),
            dma((n, 2, parts)),
            dma((n,)),
            dma((n,)),
            dma((n,)),
            dma((2,)),
            dma((parts,)),
            dma((parts,)),
            dma((2, parts)),
        ],
        compiler_params=pltpu.CompilerParams(
            collective_id=0, has_side_effects=True, vmem_limit_bytes=60 * 1024 * 1024
        ),
        cost_estimate=pl.CostEstimate(
            flops=10 * n * rows * rank * width, bytes_accessed=16 * rank * width, transcendentals=0
        ),
    )(
        stash.reshape(rows, width),
        back_in.reshape(rows, width),
        down_proj[0],
        up_proj[0],
        gain,
        sent_to,
        sent_count,
        recv_from,
        back_live,
    )
    returned, grad_down, grad_up = pl.pallas_call(
        place_kernel,
        out_shape=[jax.ShapeDtypeStruct(r.shape, r.dtype) for r in results],
        in_specs=[hbm] * 3,
        out_specs=[hbm] * 3,
        scratch_shapes=[pltpu.VMEM(r.shape, r.dtype) for r in results] + [dma((3, 3))] * 2,
        compiler_params=pltpu.CompilerParams(vmem_limit_bytes=60 * 1024 * 1024),
    )(*results)
    return returned.reshape(stash.shape), grad_down[None], grad_up[None]


def by_size(stash, *rest):
    n, sections = lax.axis_size("peer"), lax.axis_size("section")
    rows = stash.shape[2] * stash.shape[3]
    few = n * rows <= LANES and n > 2 and sections > 2
    return (gathered if few else on_device)(stash, *rest)


def solution(mesh):
    placed = (
        P("section", "peer", None, None, None),
        P("section", "peer", None, None, None),
        P("section", None, None),
        P("section", None, None),
        P("section", None),
        P("section", "peer", None),
        P("section", "peer"),
        P("section", "peer", None),
        P("section", "peer", None),
    )
    return jax.shard_map(
        by_size,
        mesh=mesh,
        in_specs=placed,
        out_specs=(
            P("section", "peer", None, None, None),
            P("section", None, None),
            P("section", None, None),
        ),
        check_vma=False,
    )
```

```python
import functools

import jax
import jax.numpy as jnp
from jax import lax
from jax.experimental import pallas as pl
from jax.experimental.pallas import tpu as pltpu
from jax.sharding import PartitionSpec as P

MESH = pl.DeviceIdType.MESH
LANES = 128
WIDE = 256

epsilon = 1e-05


def passed_along(block, axis, distance):
    devices = range(lax.axis_size(axis))
    route = [((i - distance) % len(devices), i) for i in devices]
    return lax.ppermute(block, axis, route)


def compact(blocks, targets, live_count):
    peer_count = blocks.shape[0]
    send_slots = targets.shape[0]
    peer_index = jnp.arange(peer_count, dtype=jnp.int32)
    slot_index = jnp.arange(send_slots, dtype=jnp.int32)
    selector = (
        (targets[:, None] == peer_index[None, :]) & (slot_index[:, None] < live_count)
    ).astype(jnp.bfloat16)
    flat = blocks.reshape(peer_count, -1)
    packed = jnp.dot(selector, flat, preferred_element_type=jnp.float32).astype(jnp.bfloat16)
    return packed.reshape((send_slots,) + blocks.shape[1:])


def on_device(stash, back_in, down_proj, up_proj, gain, sent_to, sent_count, recv_from, back_live):
    peer_count = lax.axis_size("peer")
    live_slots = back_live[0, 0]
    slot_mask = live_slots.astype(jnp.bfloat16)[:, None, None]
    slot_count = stash.shape[2]
    micro_rows = stash.shape[3]
    model_width = stash.shape[4]
    stored = (stash[0, 0] * slot_mask).reshape(slot_count * micro_rows, model_width)
    incoming = (back_in[0, 0] * slot_mask).reshape(slot_count * micro_rows, model_width)
    section_gain = gain[0]
    down_local = down_proj[0]
    up_local = up_proj[0]
    stored_f = stored.astype(jnp.float32)
    inverse = lax.rsqrt(jnp.mean(stored_f * stored_f, axis=-1, keepdims=True) + epsilon)
    unit_rows = stored_f * inverse
    normed = (unit_rows * section_gain).astype(jnp.bfloat16)
    contract_last = (((1,), (1,)), ((), ()))
    contract_rows = (((0,), (0,)), ((), ()))
    preact = lax.dot_general(normed, down_local, contract_last, preferred_element_type=jnp.float32)
    sigmoid_pre = jax.nn.sigmoid(preact)
    activation = (preact * sigmoid_pre).astype(jnp.bfloat16)
    back_act = lax.dot_general(
        incoming, up_local, contract_last, preferred_element_type=jnp.float32
    )
    back_pre = (back_act * (sigmoid_pre * (1.0 + preact * (1.0 - sigmoid_pre)))).astype(
        jnp.bfloat16
    )
    back_norm = jnp.dot(back_pre, down_local, preferred_element_type=jnp.float32) * section_gain
    input_grad = incoming.astype(jnp.float32) + inverse * (
        back_norm - unit_rows * jnp.mean(back_norm * unit_rows, axis=-1, keepdims=True)
    )
    input_grad = input_grad.astype(jnp.bfloat16)
    peer_index = jnp.arange(peer_count, dtype=jnp.int32)
    spreader = (
        (recv_from[0, 0][None, :] == peer_index[:, None]) & (live_slots[None, :] == 1)
    ).astype(jnp.bfloat16)
    by_sender = jnp.dot(
        spreader, input_grad.reshape(slot_count, -1), preferred_element_type=jnp.float32
    ).astype(jnp.bfloat16)
    by_sender = by_sender.reshape(peer_count, micro_rows, model_width)
    exchanged = lax.all_to_all(by_sender, "peer", split_axis=0, concat_axis=0, tiled=True)
    arrived = passed_along(exchanged, "section", -1)
    returned = compact(arrived, sent_to[0, 0], sent_count[0, 0])
    part_down = (
        lax.dot_general(back_pre, normed, contract_rows, preferred_element_type=jnp.float32)
        .astype(jnp.bfloat16)
        .astype(jnp.float32)
    )
    part_up = (
        lax.dot_general(activation, incoming, contract_rows, preferred_element_type=jnp.float32)
        .astype(jnp.bfloat16)
        .astype(jnp.float32)
    )
    summed_down, summed_up = (
        lax.psum(part_down.astype(jnp.bfloat16), "peer").astype(jnp.float32),
        lax.psum(part_up.astype(jnp.bfloat16), "peer").astype(jnp.float32),
    )
    grad_down = (summed_down / peer_count).astype(jnp.bfloat16)
    grad_up = (summed_up / peer_count).astype(jnp.bfloat16)
    return (returned[None, None], grad_down[None], grad_up[None])


def gather_kernel(
    sections,
    n,
    parts,
    stash,
    back_in,
    down,
    up,
    gain_in,
    sent_to_in,
    sent_count_in,
    recv_from_in,
    back_live_in,
    returned,
    grad_down_out,
    grad_up_out,
    rows_all,
    factors,
    w_down,
    w_up,
    asked,
    wanted,
    picked,
    grad_down,
    grad_up,
    gain_ref,
    sent_to,
    sent_count,
    recv_from,
    back_live,
    local_sem,
    right_sem,
    left_sem,
    recv_sem,
    fac_right,
    fac_left,
    fac_recv,
    want_sem,
    back_send,
    back_recv,
    out_sem,
):
    section = lax.axis_index("section")
    me = lax.axis_index("peer")
    before = lax.rem(section + sections - 1, sections)
    after = lax.rem(section + 1, sections)
    rows, width = stash.shape
    rank = down.shape[0]
    even = 4
    part = width // even
    narrow = width // (10 * LANES) * LANES
    wide = (width - narrow) // (parts - 1) // LANES * LANES
    sizes = [wide] * (parts - 1) + [width - wide * (parts - 1)]
    has_left, has_right = me > 0, me < n - 1

    def cols(j):
        return pl.ds(j * wide, sizes[j])

    def even_cols(j):
        return pl.ds(pl.multiple_of(j * part, part), part)

    def along(origin, kind, j, step, own=False):
        view = rows_all.at[origin, kind, :, cols(j)]
        source = (stash, back_in)[kind].at[:, cols(j)] if own else view
        return pltpu.make_async_remote_copy(
            src_ref=source,
            dst_ref=view,
            send_sem=(right_sem if step > 0 else left_sem).at[origin, kind, j],
            recv_sem=recv_sem.at[origin, kind, j],
            device_id=(section, me + step),
            device_id_type=MESH,
        )

    def factor_along(origin, step):
        return pltpu.make_async_remote_copy(
            src_ref=factors.at[origin],
            dst_ref=factors.at[origin],
            send_sem=(fac_right if step > 0 else fac_left).at[origin],
            recv_sem=fac_recv.at[origin],
            device_id=(section, me + step),
            device_id_type=MESH,
        )

    def want_copy():
        return pltpu.make_async_remote_copy(
            src_ref=asked,
            dst_ref=wanted,
            send_sem=want_sem.at[0],
            recv_sem=want_sem.at[1],
            device_id=(after, me),
            device_id_type=MESH,
        )

    def back_copy(j):
        return pltpu.make_async_remote_copy(
            src_ref=picked.at[:, cols(j)],
            dst_ref=returned.at[:, cols(j)],
            send_sem=back_send.at[j],
            recv_sem=back_recv.at[j],
            device_id=(before, me),
            device_id_type=MESH,
        )

    small = [
        pltpu.make_async_copy(sent_to_in, sent_to, local_sem.at[5]),
        pltpu.make_async_copy(sent_count_in, sent_count, local_sem.at[6]),
        pltpu.make_async_copy(recv_from_in, recv_from, local_sem.at[7]),
        pltpu.make_async_copy(back_live_in, back_live, local_sem.at[8]),
    ]
    def stores(j):
        return (
            pltpu.make_async_copy(
                grad_down.at[:, cols(j)], grad_down_out.at[:, cols(j)], out_sem.at[0, j]
            ),
            pltpu.make_async_copy(
                grad_up.at[:, cols(j)], grad_up_out.at[:, cols(j)], out_sem.at[1, j]
            ),
        )

    loads = [
        pltpu.make_async_copy(stash, rows_all.at[me, 0], local_sem.at[0]),
        pltpu.make_async_copy(back_in, rows_all.at[me, 1], local_sem.at[1]),
        pltpu.make_async_copy(down, w_down.at[pl.ds(0, rank)], local_sem.at[2]),
        pltpu.make_async_copy(up, w_up.at[pl.ds(0, rank)], local_sem.at[3]),
        pltpu.make_async_copy(gain_in, gain_ref, local_sem.at[4]),
    ]
    for load in small + loads:
        load.start()

    barrier = pltpu.get_barrier_semaphore()
    for other in (before, after):
        pl.semaphore_signal(barrier, inc=1, device_id=(other, me), device_id_type=MESH)

    @pl.when(has_left)
    def _():
        pl.semaphore_signal(barrier, inc=1, device_id=(section, me - 1), device_id_type=MESH)

    @pl.when(has_right)
    def _():
        pl.semaphore_signal(barrier, inc=1, device_id=(section, me + 1), device_id_type=MESH)

    @pl.when(has_left & has_right)
    def _():
        pl.semaphore_wait(barrier, 4)

    @pl.when(jnp.logical_not(has_left & has_right))
    def _():
        pl.semaphore_wait(barrier, 3)

    for j in range(parts):
        for kind in (0, 1):

            @pl.when(has_right)
            def _(j=j, kind=kind):
                along(me, kind, j, 1, True).start()

            @pl.when(has_left)
            def _(j=j, kind=kind):
                along(me, kind, j, -1, True).start()

    for load in small:
        load.wait()
    slots = sent_to.shape[2]
    micro = rows // slots
    at_row = lax.broadcasted_iota(jnp.int32, (rows, LANES), 0)
    at_lane = lax.broadcasted_iota(jnp.int32, (rows, LANES), 1)
    lane_peer = jnp.zeros((rows, LANES), jnp.int32)
    for a in range(1, n):
        lane_peer += jnp.where(at_lane >= a * rows, 1, 0)
    target = jnp.full((rows, LANES), -1, jnp.int32)
    for k in range(slots):
        here = (at_row >= k * micro) & (at_row < (k + 1) * micro)
        target = jnp.where(here & (sent_count[0, 0] > k), sent_to[0, 0, k], target)
    same = lax.rem(at_lane, micro) == lax.rem(at_row, micro)
    asked[...] = jnp.where(same & (lane_peer == target), 1.0, 0.0)
    want_copy().start()

    w_down[pl.ds(rank, WIDE - rank), :] = jnp.zeros((WIDE - rank, width), jnp.bfloat16)
    w_up[pl.ds(rank, WIDE - rank), :] = jnp.zeros((WIDE - rank, width), jnp.bfloat16)
    for load in loads:
        load.wait()

    def square_part(j, total):
        block = rows_all[me, 0, :, even_cols(j)].astype(jnp.float32)
        return total + jnp.sum(block * block, axis=-1, keepdims=True)

    squares = lax.fori_loop(0, even, square_part, jnp.zeros((rows, 1), jnp.float32))
    inverse = lax.rsqrt(squares / width + epsilon)
    contract_last = (((1,), (1,)), ((), ()))

    def project_part(j, carry):
        pre, back = carry
        block = rows_all[me, 0, :, even_cols(j)].astype(jnp.float32)
        normed = (block * inverse * gain_ref[:, even_cols(j)]).astype(jnp.bfloat16)
        pre = pre + lax.dot_general(
            normed, w_down[:, even_cols(j)], contract_last, preferred_element_type=jnp.float32
        )
        back = back + lax.dot_general(
            rows_all[me, 1, :, even_cols(j)],
            w_up[:, even_cols(j)],
            contract_last,
            preferred_element_type=jnp.float32,
        )
        return pre, back

    empty = jnp.zeros((rows, WIDE), jnp.float32)
    preact, back_act = lax.fori_loop(0, even, project_part, (empty, empty))
    row_only = lax.broadcasted_iota(jnp.int32, (rows, 1), 0)
    live = jnp.zeros((rows, 1), jnp.float32)
    code = jnp.zeros((rows, 1), jnp.float32)
    for k in range(slots):
        held = back_live[0, 0, k]
        here = (row_only >= k * micro) & (row_only < (k + 1) * micro)
        live = jnp.where(here, held.astype(jnp.float32), live)
        code = jnp.where(here, ((recv_from[0, 0, k] + 1) * held).astype(jnp.float32), code)
    sigmoid_pre = jax.nn.sigmoid(preact)
    activation = preact * sigmoid_pre * live
    back_pre = back_act * (sigmoid_pre * (1.0 + preact * (1.0 - sigmoid_pre))) * live
    slope = jnp.sum(back_pre * preact, axis=-1, keepdims=True) * (inverse * inverse / width)
    slope_high = slope.astype(jnp.bfloat16).astype(jnp.float32)
    packed = factors.shape[2]
    extra = jnp.zeros((rows, packed - WIDE), jnp.float32)
    lane = lax.broadcasted_iota(jnp.int32, (rows, packed), 1)
    body = jnp.concatenate([back_pre * inverse, extra], axis=1)
    body += pltpu.roll(jnp.concatenate([activation, extra], axis=1), rank, 1)
    for at, value in enumerate((slope_high, slope - slope_high, code)):
        body = jnp.where(lane == 2 * rank + at, value, body)
    factors[me] = body.astype(jnp.bfloat16)

    @pl.when(has_right)
    def _():
        factor_along(me, 1).start()

    @pl.when(has_left)
    def _():
        factor_along(me, -1).start()

    def arrivals(distance, j):
        for step in (1, -1):
            origin = me - step * distance
            there = (origin >= 0) if step > 0 else (origin < n)
            on = has_right if step > 0 else has_left

            @pl.when(there)
            def _(origin=origin, step=step, on=on):
                for kind in (0, 1):
                    along(origin, kind, j, step).wait_recv()

                    @pl.when(on)
                    def _(kind=kind):
                        along(origin, kind, j, step).start()

    def factor_arrivals(distance):
        for step in (1, -1):
            origin = me - step * distance
            there = (origin >= 0) if step > 0 else (origin < n)
            on = has_right if step > 0 else has_left

            @pl.when(there)
            def _(origin=origin, step=step, on=on):
                factor_along(origin, step).wait_recv()

                @pl.when(on)
                def _():
                    factor_along(origin, step).start()

    for distance in range(1, n):
        arrivals(distance, 0)
        factor_arrivals(distance)
        if distance < n - 1:
            for j in range(1, parts):
                arrivals(distance, j)

    want_copy().wait()
    body_all = jnp.concatenate([factors[a].astype(jnp.float32) for a in range(n)], axis=0)
    body_t = jnp.transpose(body_all)
    mine = (me + 1).astype(jnp.float32)
    codes_all = body_t[2 * rank + 2 : 2 * rank + 3]
    select = jnp.where(codes_all == mine, wanted[...][:, : n * rows], 0.0)
    chosen = jnp.dot(
        select.astype(jnp.bfloat16), body_all.astype(jnp.bfloat16), preferred_element_type=jnp.float32
    )
    chosen_back = chosen[:, :WIDE].astype(jnp.bfloat16)
    slope_lane = (lane == 2 * rank) | (lane == 2 * rank + 1)
    chosen_slope = jnp.sum(jnp.where(slope_lane, chosen, 0.0), axis=-1, keepdims=True)
    down_pick = jnp.concatenate([select, body_t[:rank]], axis=0).astype(jnp.bfloat16)
    up_pick = jnp.concatenate([select, body_t[rank : 2 * rank]], axis=0).astype(jnp.bfloat16)

    def finish(j):
        if j > 0:
            arrivals(n - 1, j)

        gain = gain_ref[:, cols(j)]

        def whole(kind):
            blocks = [rows_all[a, kind, :, cols(j)].astype(jnp.float32) for a in range(n)]
            return jnp.concatenate(blocks, axis=0).astype(jnp.bfloat16)

        stash_all, back_all = whole(0), whole(1)
        through = jnp.dot(chosen_back, w_down[:, cols(j)], preferred_element_type=jnp.float32)
        from_stash = jnp.dot(down_pick, stash_all, preferred_element_type=jnp.float32)
        from_back = jnp.dot(up_pick, back_all, preferred_element_type=jnp.float32)
        out = from_back[:rows] + through * gain - chosen_slope * from_stash[:rows]
        picked[:, cols(j)] = out.astype(jnp.bfloat16)
        back_copy(j).start()
        grad_down[:, cols(j)] = (from_stash[rows:] * (gain / n)).astype(jnp.bfloat16)
        grad_up[:, cols(j)] = (from_back[rows:] / n).astype(jnp.bfloat16)
        for store in stores(j):
            store.start()

    for j in range(parts):
        finish(j)

    def drain(j):
        back_copy(j).wait()
        for store in stores(j):
            store.wait()
        for kind in (0, 1):

            @pl.when(has_right)
            def _(kind=kind):
                along(me, kind, j, 1, True).wait_send()

            @pl.when(has_left)
            def _(kind=kind):
                along(me, kind, j, -1, True).wait_send()

        for distance in range(1, n):
            for step in (1, -1):
                origin = me - step * distance
                there = (origin >= 0) if step > 0 else (origin < n)
                on = has_right if step > 0 else has_left

                @pl.when(there & on)
                def _(origin=origin, step=step):
                    for kind in (0, 1):
                        along(origin, kind, j, step).wait_send()

    for j in range(parts):
        drain(j)

    for distance in range(n):
        for step in (1, -1):
            if distance == 0 or distance < n - 1:
                origin = me - step * distance
                there = (origin >= 0) if step > 0 else (origin < n)
                on = has_right if step > 0 else has_left

                @pl.when(there & on)
                def _(origin=origin, step=step):
                    factor_along(origin, step).wait_send()


def place_kernel(*refs):
    sources, targets, held, (read_sem, write_sem) = refs[:3], refs[3:6], refs[6:9], refs[9:]
    reads, writes = [], []
    for i in (1, 2, 0):
        height = sources[i].shape[0]
        pieces = 3 if height % 48 == 0 else 1
        for piece in range(pieces):
            span = pl.ds(piece * (height // pieces), height // pieces)
            inside = held[i].at[span]
            reads.append(
                pltpu.make_async_copy(sources[i].at[span], inside, read_sem.at[i, piece])
            )
            writes.append(
                pltpu.make_async_copy(inside, targets[i].at[span], write_sem.at[i, piece])
            )
    for read in reads:
        read.start()
    for read, write in zip(reads, writes):
        read.wait()
        write.start()
    for write in writes:
        write.wait()


def gathered(stash, back_in, down_proj, up_proj, gain, sent_to, sent_count, recv_from, back_live):
    sections, n = lax.axis_size("section"), lax.axis_size("peer")
    slots, micro, width = stash.shape[2:]
    rows = slots * micro
    rank = down_proj.shape[1]
    parts = 4
    packed = -(-(2 * rank + 3) // LANES) * LANES
    hbm = pl.BlockSpec(memory_space=pltpu.HBM)
    dma = pltpu.SemaphoreType.DMA
    results = pl.pallas_call(
        functools.partial(gather_kernel, sections, n, parts),
        out_shape=(
            jax.ShapeDtypeStruct((rows, width), jnp.bfloat16),
            jax.ShapeDtypeStruct((rank, width), jnp.bfloat16),
            jax.ShapeDtypeStruct((rank, width), jnp.bfloat16),
        ),
        in_specs=[hbm] * 9,
        out_specs=(hbm, hbm, hbm),
        scratch_shapes=[
            pltpu.VMEM((n, 2, rows, width), jnp.bfloat16),
            pltpu.VMEM((n, rows, packed), jnp.bfloat16),
            pltpu.VMEM((WIDE, width), jnp.bfloat16),
            pltpu.VMEM((WIDE, width), jnp.bfloat16),
            pltpu.VMEM((rows, LANES), jnp.float32),
            pltpu.VMEM((rows, LANES), jnp.float32),
            pltpu.VMEM((rows, width), jnp.bfloat16),
            pltpu.VMEM((rank, width), jnp.bfloat16),
            pltpu.VMEM((rank, width), jnp.bfloat16),
            pltpu.VMEM((1, width), jnp.float32),
            pltpu.SMEM(sent_to.shape, jnp.int32),
            pltpu.SMEM(sent_count.shape, jnp.int32),
            pltpu.SMEM(recv_from.shape, jnp.int32),
            pltpu.SMEM(back_live.shape, jnp.int32),
            dma((9,)),
            dma((n, 2, parts)),
            dma((n, 2, parts)),
            dma((n, 2, parts)),
            dma((n,)),
            dma((n,)),
            dma((n,)),
            dma((2,)),
            dma((parts,)),
            dma((parts,)),
            dma((2, parts)),
        ],
        compiler_params=pltpu.CompilerParams(
            collective_id=0, has_side_effects=True, vmem_limit_bytes=60 * 1024 * 1024
        ),
        cost_estimate=pl.CostEstimate(
            flops=10 * n * rows * rank * width, bytes_accessed=16 * rank * width, transcendentals=0
        ),
    )(
        stash.reshape(rows, width),
        back_in.reshape(rows, width),
        down_proj[0],
        up_proj[0],
        gain,
        sent_to,
        sent_count,
        recv_from,
        back_live,
    )
    returned, grad_down, grad_up = pl.pallas_call(
        place_kernel,
        out_shape=[jax.ShapeDtypeStruct(r.shape, r.dtype) for r in results],
        in_specs=[hbm] * 3,
        out_specs=[hbm] * 3,
        scratch_shapes=[pltpu.VMEM(r.shape, r.dtype) for r in results] + [dma((3, 3))] * 2,
        compiler_params=pltpu.CompilerParams(vmem_limit_bytes=60 * 1024 * 1024),
    )(*results)
    return returned.reshape(stash.shape), grad_down[None], grad_up[None]


def by_size(stash, *rest):
    n, sections = lax.axis_size("peer"), lax.axis_size("section")
    rows = stash.shape[2] * stash.shape[3]
    few = n * rows <= LANES and n > 2 and sections > 2
    return (gathered if few else on_device)(stash, *rest)


def solution(mesh):
    placed = (
        P("section", "peer", None, None, None),
        P("section", "peer", None, None, None),
        P("section", None, None),
        P("section", None, None),
        P("section", None),
        P("section", "peer", None),
        P("section", "peer"),
        P("section", "peer", None),
        P("section", "peer", None),
    )
    return jax.shard_map(
        by_size,
        mesh=mesh,
        in_specs=placed,
        out_specs=(
            P("section", "peer", None, None, None),
            P("section", None, None),
            P("section", None, None),
        ),
        check_vma=False,
    )
```

```python
import functools

import jax
import jax.numpy as jnp
from jax import lax
from jax.experimental import pallas as pl
from jax.experimental.pallas import tpu as pltpu
from jax.sharding import PartitionSpec as P

MESH = pl.DeviceIdType.MESH
LANES = 128
WIDE = 256

epsilon = 1e-05


def passed_along(block, axis, distance):
    devices = range(lax.axis_size(axis))
    route = [((i - distance) % len(devices), i) for i in devices]
    return lax.ppermute(block, axis, route)


def compact(blocks, targets, live_count):
    peer_count = blocks.shape[0]
    send_slots = targets.shape[0]
    peer_index = jnp.arange(peer_count, dtype=jnp.int32)
    slot_index = jnp.arange(send_slots, dtype=jnp.int32)
    selector = (
        (targets[:, None] == peer_index[None, :]) & (slot_index[:, None] < live_count)
    ).astype(jnp.bfloat16)
    flat = blocks.reshape(peer_count, -1)
    packed = jnp.dot(selector, flat, preferred_element_type=jnp.float32).astype(jnp.bfloat16)
    return packed.reshape((send_slots,) + blocks.shape[1:])


def on_device(stash, back_in, down_proj, up_proj, gain, sent_to, sent_count, recv_from, back_live):
    peer_count = lax.axis_size("peer")
    live_slots = back_live[0, 0]
    slot_mask = live_slots.astype(jnp.bfloat16)[:, None, None]
    slot_count = stash.shape[2]
    micro_rows = stash.shape[3]
    model_width = stash.shape[4]
    stored = (stash[0, 0] * slot_mask).reshape(slot_count * micro_rows, model_width)
    incoming = (back_in[0, 0] * slot_mask).reshape(slot_count * micro_rows, model_width)
    section_gain = gain[0]
    down_local = down_proj[0]
    up_local = up_proj[0]
    stored_f = stored.astype(jnp.float32)
    inverse = lax.rsqrt(jnp.mean(stored_f * stored_f, axis=-1, keepdims=True) + epsilon)
    unit_rows = stored_f * inverse
    normed = (unit_rows * section_gain).astype(jnp.bfloat16)
    contract_last = (((1,), (1,)), ((), ()))
    contract_rows = (((0,), (0,)), ((), ()))
    preact = lax.dot_general(normed, down_local, contract_last, preferred_element_type=jnp.float32)
    sigmoid_pre = jax.nn.sigmoid(preact)
    activation = (preact * sigmoid_pre).astype(jnp.bfloat16)
    back_act = lax.dot_general(
        incoming, up_local, contract_last, preferred_element_type=jnp.float32
    )
    back_pre = (back_act * (sigmoid_pre * (1.0 + preact * (1.0 - sigmoid_pre)))).astype(
        jnp.bfloat16
    )
    back_norm = jnp.dot(back_pre, down_local, preferred_element_type=jnp.float32) * section_gain
    input_grad = incoming.astype(jnp.float32) + inverse * (
        back_norm - unit_rows * jnp.mean(back_norm * unit_rows, axis=-1, keepdims=True)
    )
    input_grad = input_grad.astype(jnp.bfloat16)
    peer_index = jnp.arange(peer_count, dtype=jnp.int32)
    spreader = (
        (recv_from[0, 0][None, :] == peer_index[:, None]) & (live_slots[None, :] == 1)
    ).astype(jnp.bfloat16)
    by_sender = jnp.dot(
        spreader, input_grad.reshape(slot_count, -1), preferred_element_type=jnp.float32
    ).astype(jnp.bfloat16)
    by_sender = by_sender.reshape(peer_count, micro_rows, model_width)
    exchanged = lax.all_to_all(by_sender, "peer", split_axis=0, concat_axis=0, tiled=True)
    arrived = passed_along(exchanged, "section", -1)
    returned = compact(arrived, sent_to[0, 0], sent_count[0, 0])
    part_down = (
        lax.dot_general(back_pre, normed, contract_rows, preferred_element_type=jnp.float32)
        .astype(jnp.bfloat16)
        .astype(jnp.float32)
    )
    part_up = (
        lax.dot_general(activation, incoming, contract_rows, preferred_element_type=jnp.float32)
        .astype(jnp.bfloat16)
        .astype(jnp.float32)
    )
    summed_down, summed_up = (
        lax.psum(part_down.astype(jnp.bfloat16), "peer").astype(jnp.float32),
        lax.psum(part_up.astype(jnp.bfloat16), "peer").astype(jnp.float32),
    )
    grad_down = (summed_down / peer_count).astype(jnp.bfloat16)
    grad_up = (summed_up / peer_count).astype(jnp.bfloat16)
    return (returned[None, None], grad_down[None], grad_up[None])


def gather_kernel(
    sections,
    n,
    parts,
    stash,
    back_in,
    down,
    up,
    gain_in,
    sent_to_in,
    sent_count_in,
    recv_from_in,
    back_live_in,
    returned,
    grad_down_out,
    grad_up_out,
    rows_all,
    factors,
    w_down,
    w_up,
    asked,
    wanted,
    picked,
    grad_down,
    grad_up,
    gain_ref,
    sent_to,
    sent_count,
    recv_from,
    back_live,
    local_sem,
    right_sem,
    left_sem,
    recv_sem,
    fac_right,
    fac_left,
    fac_recv,
    want_sem,
    back_send,
    back_recv,
    out_sem,
):
    section = lax.axis_index("section")
    me = lax.axis_index("peer")
    before = lax.rem(section + sections - 1, sections)
    after = lax.rem(section + 1, sections)
    rows, width = stash.shape
    rank = down.shape[0]
    even = 4
    part = width // even
    narrow = width // (10 * LANES) * LANES
    wide = (width - narrow) // (parts - 1) // LANES * LANES
    sizes = [wide] * (parts - 1) + [width - wide * (parts - 1)]
    has_left, has_right = me > 0, me < n - 1

    def cols(j):
        return pl.ds(j * wide, sizes[j])

    def even_cols(j):
        return pl.ds(pl.multiple_of(j * part, part), part)

    def along(origin, kind, j, step, own=False):
        view = rows_all.at[origin, kind, :, cols(j)]
        source = (stash, back_in)[kind].at[:, cols(j)] if own else view
        return pltpu.make_async_remote_copy(
            src_ref=source,
            dst_ref=view,
            send_sem=(right_sem if step > 0 else left_sem).at[origin, kind, j],
            recv_sem=recv_sem.at[origin, kind, j],
            device_id=(section, me + step),
            device_id_type=MESH,
        )

    def factor_along(origin, step):
        return pltpu.make_async_remote_copy(
            src_ref=factors.at[origin],
            dst_ref=factors.at[origin],
            send_sem=(fac_right if step > 0 else fac_left).at[origin],
            recv_sem=fac_recv.at[origin],
            device_id=(section, me + step),
            device_id_type=MESH,
        )

    def want_copy():
        return pltpu.make_async_remote_copy(
            src_ref=asked,
            dst_ref=wanted,
            send_sem=want_sem.at[0],
            recv_sem=want_sem.at[1],
            device_id=(after, me),
            device_id_type=MESH,
        )

    def back_copy(j):
        return pltpu.make_async_remote_copy(
            src_ref=picked.at[:, cols(j)],
            dst_ref=returned.at[:, cols(j)],
            send_sem=back_send.at[j],
            recv_sem=back_recv.at[j],
            device_id=(before, me),
            device_id_type=MESH,
        )

    small = [
        pltpu.make_async_copy(sent_to_in, sent_to, local_sem.at[5]),
        pltpu.make_async_copy(sent_count_in, sent_count, local_sem.at[6]),
        pltpu.make_async_copy(recv_from_in, recv_from, local_sem.at[7]),
        pltpu.make_async_copy(back_live_in, back_live, local_sem.at[8]),
    ]
    def stores(j):
        return (
            pltpu.make_async_copy(
                grad_down.at[:, cols(j)], grad_down_out.at[:, cols(j)], out_sem.at[0, j]
            ),
            pltpu.make_async_copy(
                grad_up.at[:, cols(j)], grad_up_out.at[:, cols(j)], out_sem.at[1, j]
            ),
        )

    loads = [
        pltpu.make_async_copy(stash, rows_all.at[me, 0], local_sem.at[0]),
        pltpu.make_async_copy(back_in, rows_all.at[me, 1], local_sem.at[1]),
        pltpu.make_async_copy(down, w_down.at[pl.ds(0, rank)], local_sem.at[2]),
        pltpu.make_async_copy(up, w_up.at[pl.ds(0, rank)], local_sem.at[3]),
        pltpu.make_async_copy(gain_in, gain_ref, local_sem.at[4]),
    ]
    for load in small + loads:
        load.start()

    barrier = pltpu.get_barrier_semaphore()
    for other in (before, after):
        pl.semaphore_signal(barrier, inc=1, device_id=(other, me), device_id_type=MESH)

    @pl.when(has_left)
    def _():
        pl.semaphore_signal(barrier, inc=1, device_id=(section, me - 1), device_id_type=MESH)

    @pl.when(has_right)
    def _():
        pl.semaphore_signal(barrier, inc=1, device_id=(section, me + 1), device_id_type=MESH)

    @pl.when(has_left & has_right)
    def _():
        pl.semaphore_wait(barrier, 4)

    @pl.when(jnp.logical_not(has_left & has_right))
    def _():
        pl.semaphore_wait(barrier, 3)

    for j in range(parts):
        for kind in (0, 1):

            @pl.when(has_right)
            def _(j=j, kind=kind):
                along(me, kind, j, 1, True).start()

            @pl.when(has_left)
            def _(j=j, kind=kind):
                along(me, kind, j, -1, True).start()

    for load in small:
        load.wait()
    slots = sent_to.shape[2]
    micro = rows // slots
    at_row = lax.broadcasted_iota(jnp.int32, (rows, LANES), 0)
    at_lane = lax.broadcasted_iota(jnp.int32, (rows, LANES), 1)
    lane_peer = jnp.zeros((rows, LANES), jnp.int32)
    for a in range(1, n):
        lane_peer += jnp.where(at_lane >= a * rows, 1, 0)
    target = jnp.full((rows, LANES), -1, jnp.int32)
    for k in range(slots):
        here = (at_row >= k * micro) & (at_row < (k + 1) * micro)
        target = jnp.where(here & (sent_count[0, 0] > k), sent_to[0, 0, k], target)
    same = lax.rem(at_lane, micro) == lax.rem(at_row, micro)
    asked[...] = jnp.where(same & (lane_peer == target), 1.0, 0.0)
    want_copy().start()

    w_down[pl.ds(rank, WIDE - rank), :] = jnp.zeros((WIDE - rank, width), jnp.bfloat16)
    w_up[pl.ds(rank, WIDE - rank), :] = jnp.zeros((WIDE - rank, width), jnp.bfloat16)
    for load in loads:
        load.wait()

    def square_part(j, total):
        block = rows_all[me, 0, :, even_cols(j)].astype(jnp.float32)
        return total + jnp.sum(block * block, axis=-1, keepdims=True)

    squares = lax.fori_loop(0, even, square_part, jnp.zeros((rows, 1), jnp.float32))
    inverse = lax.rsqrt(squares / width + epsilon)
    contract_last = (((1,), (1,)), ((), ()))

    def project_part(j, carry):
        pre, back = carry
        block = rows_all[me, 0, :, even_cols(j)].astype(jnp.float32)
        normed = (block * inverse * gain_ref[:, even_cols(j)]).astype(jnp.bfloat16)
        pre = pre + lax.dot_general(
            normed, w_down[:, even_cols(j)], contract_last, preferred_element_type=jnp.float32
        )
        back = back + lax.dot_general(
            rows_all[me, 1, :, even_cols(j)],
            w_up[:, even_cols(j)],
            contract_last,
            preferred_element_type=jnp.float32,
        )
        return pre, back

    empty = jnp.zeros((rows, WIDE), jnp.float32)
    preact, back_act = lax.fori_loop(0, even, project_part, (empty, empty))
    row_only = lax.broadcasted_iota(jnp.int32, (rows, 1), 0)
    live = jnp.zeros((rows, 1), jnp.float32)
    code = jnp.zeros((rows, 1), jnp.float32)
    for k in range(slots):
        held = back_live[0, 0, k]
        here = (row_only >= k * micro) & (row_only < (k + 1) * micro)
        live = jnp.where(here, held.astype(jnp.float32), live)
        code = jnp.where(here, ((recv_from[0, 0, k] + 1) * held).astype(jnp.float32), code)
    sigmoid_pre = jax.nn.sigmoid(preact)
    activation = preact * sigmoid_pre * live
    back_pre = back_act * (sigmoid_pre * (1.0 + preact * (1.0 - sigmoid_pre))) * live
    slope = jnp.sum(back_pre * preact, axis=-1, keepdims=True) * (inverse * inverse / width)
    slope_high = slope.astype(jnp.bfloat16).astype(jnp.float32)
    packed = factors.shape[2]
    extra = jnp.zeros((rows, packed - WIDE), jnp.float32)
    lane = lax.broadcasted_iota(jnp.int32, (rows, packed), 1)
    body = jnp.concatenate([back_pre * inverse, extra], axis=1)
    body += pltpu.roll(jnp.concatenate([activation, extra], axis=1), rank, 1)
    for at, value in enumerate((slope_high, slope - slope_high, code)):
        body = jnp.where(lane == 2 * rank + at, value, body)
    factors[me] = body.astype(jnp.bfloat16)

    @pl.when(has_right)
    def _():
        factor_along(me, 1).start()

    @pl.when(has_left)
    def _():
        factor_along(me, -1).start()

    def arrivals(distance, j):
        for step in (1, -1):
            origin = me - step * distance
            there = (origin >= 0) if step > 0 else (origin < n)
            on = has_right if step > 0 else has_left

            @pl.when(there)
            def _(origin=origin, step=step, on=on):
                for kind in (0, 1):
                    along(origin, kind, j, step).wait_recv()

                    @pl.when(on)
                    def _(kind=kind):
                        along(origin, kind, j, step).start()

    def factor_arrivals(distance):
        for step in (1, -1):
            origin = me - step * distance
            there = (origin >= 0) if step > 0 else (origin < n)
            on = has_right if step > 0 else has_left

            @pl.when(there)
            def _(origin=origin, step=step, on=on):
                factor_along(origin, step).wait_recv()

                @pl.when(on)
                def _():
                    factor_along(origin, step).start()

    for distance in range(1, n):
        arrivals(distance, 0)
        factor_arrivals(distance)
        if distance < n - 1:
            for j in range(1, parts):
                arrivals(distance, j)

    want_copy().wait()
    body_all = jnp.concatenate([factors[a].astype(jnp.float32) for a in range(n)], axis=0)
    body_t = jnp.transpose(body_all)
    mine = (me + 1).astype(jnp.float32)
    codes_all = body_t[2 * rank + 2 : 2 * rank + 3]
    select = jnp.where(codes_all == mine, wanted[...][:, : n * rows], 0.0)
    chosen = jnp.dot(
        select.astype(jnp.bfloat16), body_all.astype(jnp.bfloat16), preferred_element_type=jnp.float32
    )
    chosen_back = chosen[:, :WIDE].astype(jnp.bfloat16)
    slope_lane = (lane == 2 * rank) | (lane == 2 * rank + 1)
    chosen_slope = jnp.sum(jnp.where(slope_lane, chosen, 0.0), axis=-1, keepdims=True)
    down_pick = jnp.concatenate([select, body_t[:rank]], axis=0).astype(jnp.bfloat16)
    up_pick = jnp.concatenate([select, body_t[rank : 2 * rank]], axis=0).astype(jnp.bfloat16)

    def finish(j):
        if j > 0:
            arrivals(n - 1, j)

        gain = gain_ref[:, cols(j)]

        def whole(kind):
            blocks = [rows_all[a, kind, :, cols(j)].astype(jnp.float32) for a in range(n)]
            return jnp.concatenate(blocks, axis=0).astype(jnp.bfloat16)

        stash_all, back_all = whole(0), whole(1)
        through = jnp.dot(chosen_back, w_down[:, cols(j)], preferred_element_type=jnp.float32)
        from_stash = jnp.dot(down_pick, stash_all, preferred_element_type=jnp.float32)
        from_back = jnp.dot(up_pick, back_all, preferred_element_type=jnp.float32)
        out = from_back[:rows] + through * gain - chosen_slope * from_stash[:rows]
        picked[:, cols(j)] = out.astype(jnp.bfloat16)
        back_copy(j).start()
        grad_down[:, cols(j)] = (from_stash[rows:] * (gain / n)).astype(jnp.bfloat16)
        grad_up[:, cols(j)] = (from_back[rows:] / n).astype(jnp.bfloat16)
        for store in stores(j):
            store.start()

    for j in range(parts):
        finish(j)

    def drain(j):
        back_copy(j).wait()
        for store in stores(j):
            store.wait()
        for kind in (0, 1):

            @pl.when(has_right)
            def _(kind=kind):
                along(me, kind, j, 1, True).wait_send()

            @pl.when(has_left)
            def _(kind=kind):
                along(me, kind, j, -1, True).wait_send()

        for distance in range(1, n):
            for step in (1, -1):
                origin = me - step * distance
                there = (origin >= 0) if step > 0 else (origin < n)
                on = has_right if step > 0 else has_left

                @pl.when(there & on)
                def _(origin=origin, step=step):
                    for kind in (0, 1):
                        along(origin, kind, j, step).wait_send()

    for j in range(parts):
        drain(j)

    for distance in range(n):
        for step in (1, -1):
            if distance == 0 or distance < n - 1:
                origin = me - step * distance
                there = (origin >= 0) if step > 0 else (origin < n)
                on = has_right if step > 0 else has_left

                @pl.when(there & on)
                def _(origin=origin, step=step):
                    factor_along(origin, step).wait_send()


def place_kernel(*refs):
    sources, targets, held, (read_sem, write_sem) = refs[:3], refs[3:6], refs[6:9], refs[9:]
    reads, writes = [], []
    for i in (1, 2, 0):
        height = sources[i].shape[0]
        pieces = 3 if height % 48 == 0 else 1
        for piece in range(pieces):
            span = pl.ds(piece * (height // pieces), height // pieces)
            inside = held[i].at[span]
            reads.append(
                pltpu.make_async_copy(sources[i].at[span], inside, read_sem.at[i, piece])
            )
            writes.append(
                pltpu.make_async_copy(inside, targets[i].at[span], write_sem.at[i, piece])
            )
    for read in reads:
        read.start()
    for read, write in zip(reads, writes):
        read.wait()
        write.start()
    for write in writes:
        write.wait()


def gathered(stash, back_in, down_proj, up_proj, gain, sent_to, sent_count, recv_from, back_live):
    sections, n = lax.axis_size("section"), lax.axis_size("peer")
    slots, micro, width = stash.shape[2:]
    rows = slots * micro
    rank = down_proj.shape[1]
    parts = 3
    packed = -(-(2 * rank + 3) // LANES) * LANES
    hbm = pl.BlockSpec(memory_space=pltpu.HBM)
    dma = pltpu.SemaphoreType.DMA
    results = pl.pallas_call(
        functools.partial(gather_kernel, sections, n, parts),
        out_shape=(
            jax.ShapeDtypeStruct((rows, width), jnp.bfloat16),
            jax.ShapeDtypeStruct((rank, width), jnp.bfloat16),
            jax.ShapeDtypeStruct((rank, width), jnp.bfloat16),
        ),
        in_specs=[hbm] * 9,
        out_specs=(hbm, hbm, hbm),
        scratch_shapes=[
            pltpu.VMEM((n, 2, rows, width), jnp.bfloat16),
            pltpu.VMEM((n, rows, packed), jnp.bfloat16),
            pltpu.VMEM((WIDE, width), jnp.bfloat16),
            pltpu.VMEM((WIDE, width), jnp.bfloat16),
            pltpu.VMEM((rows, LANES), jnp.float32),
            pltpu.VMEM((rows, LANES), jnp.float32),
            pltpu.VMEM((rows, width), jnp.bfloat16),
            pltpu.VMEM((rank, width), jnp.bfloat16),
            pltpu.VMEM((rank, width), jnp.bfloat16),
            pltpu.VMEM((1, width), jnp.float32),
            pltpu.SMEM(sent_to.shape, jnp.int32),
            pltpu.SMEM(sent_count.shape, jnp.int32),
            pltpu.SMEM(recv_from.shape, jnp.int32),
            pltpu.SMEM(back_live.shape, jnp.int32),
            dma((9,)),
            dma((n, 2, parts)),
            dma((n, 2, parts)),
            dma((n, 2, parts)),
            dma((n,)),
            dma((n,)),
            dma((n,)),
            dma((2,)),
            dma((parts,)),
            dma((parts,)),
            dma((2, parts)),
        ],
        compiler_params=pltpu.CompilerParams(
            collective_id=0, has_side_effects=True, vmem_limit_bytes=60 * 1024 * 1024
        ),
        cost_estimate=pl.CostEstimate(
            flops=10 * n * rows * rank * width, bytes_accessed=16 * rank * width, transcendentals=0
        ),
    )(
        stash.reshape(rows, width),
        back_in.reshape(rows, width),
        down_proj[0],
        up_proj[0],
        gain,
        sent_to,
        sent_count,
        recv_from,
        back_live,
    )
    returned, grad_down, grad_up = pl.pallas_call(
        place_kernel,
        out_shape=[jax.ShapeDtypeStruct(r.shape, r.dtype) for r in results],
        in_specs=[hbm] * 3,
        out_specs=[hbm] * 3,
        scratch_shapes=[pltpu.VMEM(r.shape, r.dtype) for r in results] + [dma((3, 3))] * 2,
        compiler_params=pltpu.CompilerParams(vmem_limit_bytes=60 * 1024 * 1024),
    )(*results)
    return returned.reshape(stash.shape), grad_down[None], grad_up[None]


def by_size(stash, *rest):
    n, sections = lax.axis_size("peer"), lax.axis_size("section")
    rows = stash.shape[2] * stash.shape[3]
    few = n * rows <= LANES and n > 2 and sections > 2
    return (gathered if few else on_device)(stash, *rest)


def solution(mesh):
    placed = (
        P("section", "peer", None, None, None),
        P("section", "peer", None, None, None),
        P("section", None, None),
        P("section", None, None),
        P("section", None),
        P("section", "peer", None),
        P("section", "peer"),
        P("section", "peer", None),
        P("section", "peer", None),
    )
    return jax.shard_map(
        by_size,
        mesh=mesh,
        in_specs=placed,
        out_specs=(
            P("section", "peer", None, None, None),
            P("section", None, None),
            P("section", None, None),
        ),
        check_vma=False,
    )
```
